32 devices in a mesh: user: 16 (over z, y, core), item: 2 (over x).
Axes of the slice: x: 2, y: 2, z: 4, core: 2. Of those that a mesh axis runs over, the one named last changes fastest.
Arguments:
- tile_vals: bfloat16 [16, 2, 128, 128, 128], P('user', 'item'), may hold values from -6 to 6
- tile_row: int32 [16, 2, 128], P('user', 'item'), may hold values from 0 to 15, as said below
- tile_col: int32 [16, 2, 128], P('user', 'item'), may hold values from 0 to 15
- tile_count: int32 [16, 2], P('user', 'item'), may hold values from 16 to 128, as said below
- fac_a: bfloat16 [64, 32768], P(None, 'user'), may hold values from -2.5 to 2.5
- fac_b: bfloat16 [64, 4096], P(None, ('item', 'user')), may hold values from -2.5 to 2.5
- omega: bfloat16 [64, 4096], P(None, ('item', 'user')), may hold values from -6 to 6
Outputs:
- user_dir: float32 [64, 32768], P(None, 'user')
- item_dir: float32 [64, 4096], P(None, ('item', 'user'))
- row_loss: float32 [16, 2, 128, 128], P('user', 'item')
The draws below stay inside these ranges and needn't reach their ends.
Inputs may be any that keep to these rules, and one draw needn't show every extreme that they name: `tile_count`: slot s of a device is used when s is under its count. Counts tend to grow with the user index, and some device of the last user index has all 128 slots used. The slots of one device name distinct (tile_row, tile_col) pairs.
All inputs are finite; a program needn't handle non-finite values.
Results may differ from the reference program's by a relative error of at most 0.0055.
Values may be sent and summed in bfloat16 or wider, within the bound.
No kernel may reach another device: no remote copies, remote signals or barrier semaphores. Data moves between devices by JAX's collectives and lax.ppermute only.
A program may use at most 64 MiB of HBM per device.

```python
import math
import jax
import jax.numpy as jnp
from jax import lax

TILE = 128
RANK = 64
ITERS = 2
U_DEV = 2048
I_DEV = 2048
CAP = 128
USERS = 32768
ITEMS = 4096
N_USER = 16
N_ITEM = 2


def tile_cells(key):
    keys = jax.random.split(key, N_USER * N_ITEM)
    cell_count = U_DEV // TILE * (I_DEV // TILE)

    def pick_cells(device_key):
        return jax.random.permutation(device_key, cell_count)[:CAP]
    return jax.vmap(pick_cells)(keys).reshape(N_USER, N_ITEM, CAP).astype(jnp.int32)


def draw_tile_row(key, part):
    cells = tile_cells(key)
    return (cells // (I_DEV // TILE)).astype(jnp.int32)


def draw_tile_col(key, part):
    cells = tile_cells(key)
    return (cells % (I_DEV // TILE)).astype(jnp.int32)


def draw_tile_count(key, part):
    key = jax.random.fold_in(key, 3)
    first_key, second_key = jax.random.split(key)
    lowest = CAP // 8
    user_ids = jnp.arange(N_USER, dtype=jnp.int32)
    rising = lowest + (CAP - lowest) * user_ids * user_ids // max((N_USER - 1) * (N_USER - 1), 1)
    jitter = jax.random.randint(first_key, (N_USER, N_ITEM), 0, CAP // 8 + 1)
    counts = jnp.maximum(rising[:, None] - jitter, lowest)
    chosen = jax.random.randint(second_key, (), 0, N_ITEM)
    fullest = (user_ids[:, None] == N_USER - 1) & (jnp.arange(N_ITEM, dtype=jnp.int32)[None, :] == chosen)
    return jnp.where(fullest, CAP, counts).astype(jnp.int32)


def level_of(key, extent, pieces, low, top_value):
    factor_of, own = 1.0, jax.random.fold_in(key, 6)
    for axis_at, blocks in pieces:
        draws = jnp.exp(jax.random.uniform(jax.random.fold_in(own, axis_at), (blocks,), jnp.float32, low / len(pieces), top_value / len(pieces)))
        factor_of = factor_of * jnp.repeat(draws, extent[axis_at] // blocks).reshape([-1 if axis == axis_at else 1 for axis in range(len(extent))])
    return factor_of


def centred(key, dims, width, bound, cuts=(), kind=jnp.bfloat16):
    entries = jax.random.normal(key, dims, jnp.float32) * width
    if len(cuts) > 0:
        entries = level_of(key, dims, cuts, -0.22, 0.18) * entries
    return jnp.clip(entries, min=-bound, max=bound).astype(kind)


def setup_inputs(seed: int = 0) -> dict:
    seeds = jax.random.split(jax.random.key(seed), 8)
    return {
        "tile_vals": centred(seeds[0], (N_USER, N_ITEM, CAP, TILE, TILE), 1.0, 6.0, ((0, 16), (1, 2))),
        "tile_row": draw_tile_row(jax.random.fold_in(seeds[7], 71), 0),
        "tile_col": draw_tile_col(jax.random.fold_in(seeds[7], 71), 0),
        "tile_count": draw_tile_count(jax.random.fold_in(seeds[7], 71), 0),
        "fac_a": centred(seeds[4], (RANK, USERS), 0.35, 2.5, ((1, 16),)),
        "fac_b": centred(seeds[5], (RANK, ITEMS), 0.35, 2.5, ((1, 32),)),
        "omega": centred(seeds[6], (RANK, ITEMS), 1.0, 6.0, ((1, 32),)),
    }


def tiles_of(mat):
    return mat.reshape(mat.shape[0], -1, TILE).transpose(1, 0, 2)

def untile(stack):
    return stack.transpose(1, 0, 2).reshape(stack.shape[1], -1)

def orthonormal(mat):
    gram = jnp.dot(mat, mat.T, precision=lax.Precision.HIGHEST)
    chol = jnp.linalg.cholesky(gram)
    inverse = lax.linalg.triangular_solve(chol, jnp.eye(RANK, dtype=mat.dtype), left_side=True, lower=True)
    return jnp.dot(inverse, mat, precision=lax.Precision.HIGHEST)

def reference(tile_vals, tile_row, tile_col, tile_count, fac_a, fac_b, omega):
    user_tiles = U_DEV // TILE
    item_tiles = I_DEV // TILE
    valid = (jnp.arange(CAP, dtype=jnp.int32)[None, None, :] < tile_count[:, :, None]).astype(jnp.float32)
    urow = (tile_row + (jnp.arange(N_USER, dtype=jnp.int32) * user_tiles)[:, None, None]).astype(jnp.int32)
    icol = (tile_col + (jnp.arange(N_ITEM, dtype=jnp.int32) * item_tiles)[None, :, None]).astype(jnp.int32)
    a_tiles = tiles_of(fac_a.astype(jnp.float32))
    b_tiles = tiles_of(fac_b.astype(jnp.float32))
    user_ids = jnp.arange(N_USER, dtype=jnp.int32)

    def predict(index):
        return jnp.einsum('nckr,ncki->ncri', a_tiles[urow[index]], b_tiles[icol[index]])

    def residual(index):
        pred = predict(index)
        return ((pred - tile_vals[index].astype(jnp.float32)) * valid[index][:, :, None, None]).astype(jnp.bfloat16)
    resid = lax.map(residual, user_ids)
    q_mat = omega
    y_hat = None
    for step in range(ITERS):
        q_tiles = tiles_of(q_mat.astype(jnp.float32))

        def user_part(index):
            part = jnp.einsum('ncki,ncri->nckr', q_tiles[icol[index]], resid[index].astype(jnp.float32))
            return jax.ops.segment_sum(part.reshape(-1, RANK, TILE), tile_row[index].reshape(-1), num_segments=user_tiles)
        y_mat = untile(lax.map(user_part, user_ids).reshape(N_USER * user_tiles, RANK, TILE))
        y_hat = orthonormal(y_mat).astype(jnp.bfloat16)
        y_tiles = tiles_of(y_hat.astype(jnp.float32))

        def item_part(total, index):
            part = jnp.einsum('nckr,ncri->ncki', y_tiles[urow[index]], resid[index].astype(jnp.float32))
            added = jax.ops.segment_sum(part.reshape(-1, RANK, TILE), icol[index].reshape(-1), num_segments=N_ITEM * item_tiles)
            return (total + added, None)
        z_tiles, _ = lax.scan(item_part, jnp.zeros((N_ITEM * item_tiles, RANK, TILE), jnp.float32), user_ids)
        q_mat = orthonormal(untile(z_tiles)).astype(jnp.bfloat16)
    y_last = tiles_of(y_hat.astype(jnp.float32))
    q_last = tiles_of(q_mat.astype(jnp.float32))
    radius = math.sqrt(USERS * ITEMS / RANK)

    def losses(index):
        pred = predict(index)
        atom = jnp.einsum('nckr,ncki->ncri', y_last[urow[index]], q_last[icol[index]])
        fresh = 0.5 * pred - 0.5 * radius * atom - tile_vals[index].astype(jnp.float32)
        return lax.optimization_barrier(jnp.mean(fresh * fresh, axis=-1)) * valid[index][:, :, None]
    row_loss = lax.map(losses, user_ids)
    user_dir = y_hat.astype(jnp.float32) * math.sqrt(USERS)
    item_dir = q_mat.astype(jnp.float32) * math.sqrt(ITEMS)
    return (user_dir, item_dir, row_loss)
```

```python
import functools
import math

import jax
import jax.numpy as jnp
from jax import lax
from jax.experimental import pallas as pl
from jax.experimental.pallas import tpu as pltpu
from jax.sharding import PartitionSpec as P

ITERS = 2
F32 = jnp.float32
BF16 = jnp.bfloat16
VMEM = pl.BlockSpec(memory_space=pltpu.VMEM)
SMEM = pl.BlockSpec(memory_space=pltpu.SMEM)
NT = (((1,), (1,)), ((), ()))
NN = (((1,), (0,)), ((), ()))


def params():
    return pltpu.CompilerParams(vmem_limit_bytes=16 * 1024 * 1024)


def xor_pairs(size, mask):
    return [(i, i ^ mask) for i in range(size)]


def bit_groups(size):
    bits = size.bit_length() - 1
    groups, at = [], 0
    while at < bits:
        width = 1 if at < 2 else min(2, bits - at)
        groups.append((at, width))
        at += width
    return groups


def position_of(index, size):
    place = index * 0
    for at, width in bit_groups(size):
        place = place * (1 << width) + ((index >> at) & ((1 << width) - 1))
    return place


def gather_blocks(held, axis, size, groups):
    for at, width in reversed(groups):
        got = [held]
        for k in range(1, 1 << width):
            got.append(lax.ppermute(held, axis, xor_pairs(size, k << at)))
        held = jnp.concatenate(got, axis=0)
    return held


def reduce_blocks(parts, axis, size):
    groups = bit_groups(size)
    for at, width in groups[:-1]:
        ways = 1 << width
        pieces = parts.reshape((ways, parts.shape[0] // ways) + parts.shape[1:])
        total = pieces[0].astype(F32)
        got = [
            lax.ppermute(pieces[k].astype(BF16), axis, xor_pairs(size, k << at))
            for k in range(1, ways)
        ]
        for piece in got:
            total = total + piece.astype(F32)
        parts = total
    at, width = groups[-1]
    mine = parts.astype(BF16)
    total = mine.astype(F32)
    got = [lax.ppermute(mine, axis, xor_pairs(size, k << at)) for k in range(1, 1 << width)]
    for k, piece in enumerate(got, 1):
        total = total + jnp.stack([piece[j ^ k] for j in range(1 << width)]).astype(F32)
    return total


def y_pass(q_cat, r_ref, y_ref):
    users = r_ref.shape[0]
    step = min(256, users)

    def body(i, carry):
        at = pl.multiple_of(i * step, step)
        y = lax.dot_general(
            q_cat, r_ref[pl.ds(at, step), :], NT, preferred_element_type=F32
        )
        y_ref[:, pl.ds(at, step)] = y.astype(y_ref.dtype)
        return carry

    lax.fori_loop(0, users // step, body, 0)


def cat_tiles(ref, rows):
    return jnp.concatenate([ref[t, rows, :] for t in range(ref.shape[0])], axis=1)


def first_kernel(count_ref, row_ref, pos_ref, vals_ref, at_ref, bq_ref, r_ref, y_ref):
    tile = vals_ref.shape[1]
    rank = bq_ref.shape[1] // 2
    users = r_ref.shape[0]
    count = count_ref[0]

    def clear(i, carry):
        r_ref[pl.ds(pl.multiple_of(i * tile, tile), tile), :] = jnp.zeros(
            (tile, r_ref.shape[1]), BF16
        )
        return carry

    lax.fori_loop(0, users // tile, clear, 0)
    group = 4

    def body(i, carry):
        for j in range(group):
            slot = i * group + j
            row = pl.multiple_of(row_ref[slot] * tile, tile)
            pos = pos_ref[slot]
            pred = lax.dot_general(
                at_ref[pl.ds(row, tile), :],
                bq_ref[pos, :rank, :],
                NN,
                preferred_element_type=F32,
            )
            kept = jnp.where(slot < count, 1.0, 0.0)
            resid = (pred - vals_ref[slot].astype(F32)) * kept
            r_ref[pl.ds(row, tile), pl.ds(pl.multiple_of(pos * tile, tile), tile)] = resid.astype(
                BF16
            )
        return carry

    lax.fori_loop(0, (count + group - 1) // group, body, 0)
    y_pass(cat_tiles(bq_ref, slice(rank, 2 * rank)), r_ref, y_ref)


def z_kernel(ya_ref, yb_ref, r_ref, z_ref):
    tile = z_ref.shape[2]
    y = (ya_ref[...].astype(F32) + yb_ref[...].astype(F32)).astype(BF16)
    wide = 2

    def body(i, carry):
        at = pl.multiple_of(i * tile * wide, tile * wide)
        z = lax.dot_general(y, r_ref[:, pl.ds(at, tile * wide)], NN, preferred_element_type=F32)
        for j in range(wide):
            z_ref[i * wide + j] = z[:, j * tile : (j + 1) * tile].astype(z_ref.dtype)
        return carry

    lax.fori_loop(0, z_ref.shape[0] // wide, body, 0)


def gram_kernel(z_ref, g_ref):
    z = cat_tiles(z_ref, slice(None))
    g_ref[...] = lax.dot_general(z, z, NT, preferred_element_type=F32)


def grams_kernel(old_ref, z_ref, g_ref):
    z = cat_tiles(z_ref, slice(None))
    old = cat_tiles(old_ref, slice(None))
    both = jnp.concatenate([z, old], axis=0)
    g_ref[...] = lax.dot_general(both, z, NT, preferred_element_type=F32)


def chol_inverse(grams):
    rank = grams[0].shape[0]
    wide = 8
    blocks = rank // wide
    rows = lax.broadcasted_iota(jnp.int32, (wide, 2 * rank), 0)
    lanes = lax.broadcasted_iota(jnp.int32, (wide, 2 * rank), 1)
    mats = []
    for g in grams:
        padded = jnp.concatenate([g, jnp.zeros_like(g)], axis=1)
        mats.append(
            [
                jnp.where(lanes == rows + (rank + i * wide), 1.0, padded[i * wide : (i + 1) * wide])
                for i in range(blocks)
            ]
        )
    for p in range(blocks):
        below = range(p, blocks)
        cols = [
            [
                {
                    i: jnp.broadcast_to(
                        mat[i][:, p * wide + k : p * wide + k + 1], (wide, 2 * rank)
                    )
                    for i in below
                }
                for k in range(wide)
            ]
            for mat in mats
        ]
        for k in range(wide):
            for mat, col in zip(mats, cols):
                inverse = 1.0 / col[k][p][k : k + 1, :]
                row = mat[p][k : k + 1, :] * inverse
                factor = {
                    i: jnp.where(rows > k, col[k][i], 0.0) if i == p else col[k][i] for i in below
                }
                heads = {q: col[q][p][k : k + 1, :] * inverse for q in range(k + 1, wide)}
                for i in below:
                    mat[i] = mat[i] - factor[i] * row
                    for q in range(k + 1, wide):
                        col[q][i] = col[q][i] - factor[i] * heads[q]
    result = []
    for mat in mats:
        out = []
        for i in range(blocks):
            diagonal = jnp.sum(
                jnp.where(lanes == rows + i * wide, mat[i], 0.0), axis=1, keepdims=True
            )
            out.append(mat[i][:, rank:] * lax.rsqrt(diagonal))
        result.append(jnp.concatenate(out, axis=0))
    return result


def two_parts(mat):
    high = mat.astype(BF16)
    return high, (mat - high.astype(F32)).astype(BF16)


def apply_inverse(inverse, mat):
    high, low = two_parts(inverse)
    return lax.dot_general(
        jnp.concatenate([high, low], axis=1),
        jnp.concatenate([mat, mat], axis=0),
        NN,
        preferred_element_type=F32,
    )


def apply_wide(inverse, mat):
    high, low = two_parts(inverse)
    part, rest = two_parts(mat)
    return lax.dot_general(
        jnp.concatenate([high, low, high], axis=1),
        jnp.concatenate([part, part, rest], axis=0),
        NN,
        preferred_element_type=F32,
    )


def y_kernel(z_ref, r_ref, y_ref):
    y_pass(cat_tiles(z_ref, slice(None)), r_ref, y_ref)


def scale_kernel(ga_ref, gb_ref, y_ref, inv_ref, out_ref):
    (inverse,) = chol_inverse([ga_ref[...] + gb_ref[...]])
    inv_ref[...] = inverse
    out_ref[...] = apply_wide(inverse, y_ref[...]).astype(BF16)


def last_kernel(
    radius,
    user_scale,
    item_scale,
    count_ref,
    row_ref,
    pos_ref,
    ga_ref,
    gb_ref,
    inv_ref,
    z_ref,
    share_ref,
    ya_ref,
    yb_ref,
    vals_ref,
    at_ref,
    bq_ref,
    user_ref,
    item_ref,
    loss_ref,
    left,
    right,
):
    tile = vals_ref.shape[1]
    rank = z_ref.shape[1]
    count = count_ref[0]
    gram = ga_ref[...] + gb_ref[...]
    y_gram = lax.dot_general(
        inv_ref[...], gram[rank:], NN, precision=lax.Precision.HIGHEST, preferred_element_type=F32
    )
    z_inv, y_inv = chol_inverse([gram[:rank], y_gram])
    for t in range(z_ref.shape[0]):
        q = apply_inverse(z_inv, z_ref[t]).astype(BF16)
        right[t, :rank] = bq_ref[t, :rank, :]
        right[t, rank : 2 * rank] = q
        right[t, 2 * rank : 3 * rank] = q
    for t in range(user_ref.shape[1] // tile):
        cols = slice(t * tile, (t + 1) * tile)
        y = ya_ref[:, cols].astype(F32) + yb_ref[:, cols].astype(F32)
        y_hat = apply_wide(y_inv, y)
        user_ref[:, cols] = y_hat * user_scale
        y_hat = y_hat.astype(BF16).astype(F32)
        turned = (y_hat * (-0.5 * radius)).T
        high, low = two_parts(turned)
        half = at_ref[cols, :].astype(F32) * 0.5
        left[cols, :] = jnp.concatenate([half.astype(BF16), high, low], axis=1)
    item_ref[...] = apply_wide(z_inv, share_ref[...]) * item_scale
    loss_ref[...] = jnp.zeros_like(loss_ref)
    group = 8
    ones = jnp.ones((group, tile), BF16)
    place = lax.broadcasted_iota(jnp.int32, (group, tile), 0)

    def body(i, carry):
        at = pl.multiple_of(i * group, group)
        total = jnp.zeros((group, tile), F32)
        for j in range(group):
            slot = at + j
            row = pl.multiple_of(row_ref[slot] * tile, tile)
            fresh = lax.dot_general(
                left[pl.ds(row, tile), :], right[pos_ref[slot]], NN, preferred_element_type=F32
            )
            fresh = fresh - vals_ref[slot].astype(F32)
            sums = lax.dot_general(
                ones, (fresh * fresh).astype(BF16), NT, preferred_element_type=F32
            )
            total = jnp.where((place == j) & (slot < count), sums, total)
        loss_ref[pl.ds(at, group), :] = total * (1.0 / tile)
        return carry

    lax.fori_loop(0, (count + group - 1) // group, body, 0)


def shards(tile_vals, tile_row, tile_col, tile_count, fac_a, fac_b, omega):
    ratings = tile_vals[0, 0]
    rows = tile_row[0, 0]
    cols = tile_col[0, 0]
    count = tile_count[0]
    cap, tile, _ = ratings.shape
    rank, users_dev = fac_a.shape
    share = fac_b.shape[1]
    n_user = lax.axis_size("user")
    n_item = lax.axis_size("item")
    items_dev = share * n_user
    item_tiles = items_dev // tile
    users, items = users_dev * n_user, items_dev * n_item
    radius = math.sqrt(users * items / rank)
    me = lax.axis_index("user").astype(jnp.int32)

    by_tile = share == tile
    slots = jnp.arange(n_user, dtype=jnp.int32)
    if by_tile:
        places = position_of(cols ^ me, n_user)
    else:
        places = cols
        order = position_of(slots ^ me, n_user)

    def to_tiles(blocks):
        if by_tile:
            return blocks
        blocks = blocks[order]
        wide = blocks.transpose(1, 0, 2).reshape(blocks.shape[1], item_tiles, tile)
        return wide.transpose(1, 0, 2)

    def to_blocks(tiles):
        if by_tile:
            return tiles
        wide = tiles.transpose(1, 0, 2).reshape(tiles.shape[1], n_user, share)
        return jnp.zeros((n_user, tiles.shape[1], share), tiles.dtype).at[order].set(
            wide.transpose(1, 0, 2)
        )

    def across(mine):
        bit = 1
        while True:
            other = lax.ppermute(mine, "item", xor_pairs(n_item, bit))
            bit *= 2
            if bit >= n_item:
                return mine, other
            mine = (mine.astype(F32) + other.astype(F32)).astype(mine.dtype)

    def reduced(parts):
        total = reduce_blocks(to_blocks(parts), "user", n_user)
        groups = bit_groups(n_user)[:-1]
        return to_tiles(gather_blocks(total.astype(BF16), "user", n_user, groups)), total[0]

    a_t = fac_a.T
    both = jnp.concatenate([fac_b, omega], axis=0)
    bq = to_tiles(gather_blocks(both[None], "user", n_user, bit_groups(n_user)))

    z_call = pl.pallas_call(
        z_kernel,
        out_shape=jax.ShapeDtypeStruct((item_tiles, rank, tile), BF16),
        in_specs=[VMEM] * 3,
        out_specs=VMEM,
        compiler_params=params(),
        name="z_pass",
    )
    resid, y_part = pl.pallas_call(
        first_kernel,
        out_shape=(
            jax.ShapeDtypeStruct((users_dev, items_dev), BF16),
            jax.ShapeDtypeStruct((rank, users_dev), BF16),
        ),
        in_specs=[SMEM] * 3 + [VMEM] * 3,
        out_specs=(VMEM, VMEM),
        compiler_params=params(),
        name="resid_y",
    )(count, rows, places, ratings, a_t, bq)
    old, _ = reduced(z_call(*across(y_part), resid))
    gram = pl.pallas_call(
        gram_kernel,
        out_shape=jax.ShapeDtypeStruct((rank, rank), F32),
        in_specs=[VMEM],
        out_specs=VMEM,
        compiler_params=params(),
        name="gram",
    )(old)
    gram_mine, gram_other = across(gram)
    y_part = pl.pallas_call(
        y_kernel,
        out_shape=jax.ShapeDtypeStruct((rank, users_dev), F32),
        in_specs=[VMEM] * 2,
        out_specs=VMEM,
        compiler_params=params(),
        cost_estimate=pl.CostEstimate(
            flops=2 * rank * users_dev * items_dev, bytes_accessed=8 << 20, transcendentals=0
        ),
        name="y_pass",
    )(old, resid)
    inverse, y_part = pl.pallas_call(
        scale_kernel,
        out_shape=(
            jax.ShapeDtypeStruct((rank, rank), F32),
            jax.ShapeDtypeStruct((rank, users_dev), BF16),
        ),
        in_specs=[VMEM] * 3,
        out_specs=(VMEM, VMEM),
        compiler_params=params(),
        name="scale_y",
    )(gram_mine, gram_other, y_part)
    y_mine, y_other = across(y_part)
    z, z_share = reduced(z_call(y_mine, y_other, resid))
    grams = pl.pallas_call(
        grams_kernel,
        out_shape=jax.ShapeDtypeStruct((2 * rank, rank), F32),
        in_specs=[VMEM] * 2,
        out_specs=VMEM,
        compiler_params=params(),
        name="grams",
    )(old, z)
    user_dir, item_dir, losses = pl.pallas_call(
        functools.partial(last_kernel, radius, math.sqrt(users), math.sqrt(items)),
        out_shape=(
            jax.ShapeDtypeStruct((rank, users_dev), F32),
            jax.ShapeDtypeStruct((rank, share), F32),
            jax.ShapeDtypeStruct((cap, tile), F32),
        ),
        in_specs=[SMEM] * 3 + [VMEM] * 10,
        out_specs=(VMEM, VMEM, VMEM),
        scratch_shapes=[
            pltpu.VMEM((users_dev, 3 * rank), BF16),
            pltpu.VMEM((item_tiles, 3 * rank, tile), BF16),
        ],
        compiler_params=params(),
        name="loss",
    )(count, rows, places, *across(grams), inverse, z, z_share, y_mine, y_other, ratings, a_t, bq)
    return (user_dir, item_dir, losses[None, None])


def solution(mesh):
    return jax.shard_map(
        shards,
        mesh=mesh,
        in_specs=(
            P("user", "item", None, None, None),
            P("user", "item", None),
            P("user", "item", None),
            P("user", "item"),
            P(None, "user"),
            P(None, ("item", "user")),
            P(None, ("item", "user")),
        ),
        out_specs=(P(None, "user"), P(None, ("item", "user")), P("user", "item", None, None)),
        check_vma=False,
    )
```

```python
import functools
import math

import jax
import jax.numpy as jnp
from jax import lax
from jax.experimental import pallas as pl
from jax.experimental.pallas import tpu as pltpu
from jax.sharding import PartitionSpec as P

ITERS = 2
F32 = jnp.float32
BF16 = jnp.bfloat16
VMEM = pl.BlockSpec(memory_space=pltpu.VMEM)
SMEM = pl.BlockSpec(memory_space=pltpu.SMEM)
NT = (((1,), (1,)), ((), ()))
NN = (((1,), (0,)), ((), ()))


def xor_pairs(size, mask):
    return [(i, i ^ mask) for i in range(size)]


def bit_groups(size):
    bits = size.bit_length() - 1
    groups, at = [], 0
    while at < bits:
        width = 1 if at < 2 else min(2, bits - at)
        groups.append((at, width))
        at += width
    return groups


def position_of(index, size):
    place = index * 0
    for at, width in bit_groups(size):
        place = place * (1 << width) + ((index >> at) & ((1 << width) - 1))
    return place


def gather_blocks(held, axis, size, groups, before=None):
    for number, (at, width) in enumerate(reversed(groups)):
        if before is not None:
            held = before(number - len(groups), held)
        got = [held]
        for k in range(1, 1 << width):
            got.append(lax.ppermute(held, axis, xor_pairs(size, k << at)))
        held = jnp.concatenate(got, axis=0)
    return held


def reduce_blocks(near, far, axis, size):
    groups = bit_groups(size)
    other = lax.ppermute(far.astype(BF16), axis, xor_pairs(size, 1))
    parts = near.astype(F32) + other.astype(F32)
    for at, width in groups[1:-1]:
        ways = 1 << width
        pieces = parts.reshape((ways, parts.shape[0] // ways) + parts.shape[1:])
        total = pieces[0].astype(F32)
        got = [
            lax.ppermute(pieces[k].astype(BF16), axis, xor_pairs(size, k << at))
            for k in range(1, ways)
        ]
        for piece in got:
            total = total + piece.astype(F32)
        parts = total
    at, width = groups[-1]
    mine = parts.astype(BF16)
    total = mine.astype(F32)
    got = [lax.ppermute(mine, axis, xor_pairs(size, k << at)) for k in range(1, 1 << width)]
    for k, piece in enumerate(got, 1):
        total = total + jnp.stack([piece[j ^ k] for j in range(1 << width)]).astype(F32)
    return total


def y_of(q_cat, r_ref, at, users):
    return lax.dot_general(
        q_cat, r_ref[at : at + users, :], NT, preferred_element_type=F32
    )


def cat_tiles(ref, rows):
    return jnp.concatenate([ref[t, rows, :] for t in range(ref.shape[0])], axis=1)


def prepare_kernel(a_ref, at_ref, r_ref):
    tile = 128

    def clear(i, carry):
        r_ref[pl.ds(pl.multiple_of(i * tile, tile), tile), :] = jnp.zeros(
            (tile, r_ref.shape[1]), BF16
        )
        return carry

    lax.fori_loop(0, r_ref.shape[0] // tile, clear, 0)
    for t in range(at_ref.shape[0] // tile):
        cols = slice(t * tile, (t + 1) * tile)
        at_ref[cols, :] = a_ref[:, cols].astype(F32).T.astype(BF16)


def first_kernel(slot_ref, vals_ref, at_ref, bq_ref, _, r_ref, y_ref):
    tile = vals_ref.shape[1]
    rank = bq_ref.shape[1] // 2
    count = slot_ref[2, 0]
    group = math.gcd(vals_ref.shape[0], 32)

    def body(i, carry):
        for j in range(group):
            slot = i * group + j
            row = pl.multiple_of(slot_ref[0, slot] * tile, tile)
            pos = slot_ref[1, slot]
            pred = lax.dot_general(
                at_ref[pl.ds(row, tile), :],
                bq_ref[pos, :rank, :],
                NN,
                preferred_element_type=F32,
            )
            kept = jnp.where(slot < count, 1.0, 0.0)
            resid = (pred - vals_ref[slot].astype(F32)) * kept
            r_ref[pl.ds(row, tile), pl.ds(pl.multiple_of(pos * tile, tile), tile)] = resid.astype(
                BF16
            )
        return carry

    lax.fori_loop(0, (count + group - 1) // group, body, 0)
    y_ref[...] = y_of(cat_tiles(bq_ref, slice(rank, 2 * rank)), r_ref, 0, y_ref.shape[1]).astype(
        BF16
    )


def omega_kernel(at, bq_ref, r_ref, y_ref):
    rank = bq_ref.shape[1] // 2
    y_ref[...] = y_of(cat_tiles(bq_ref, slice(rank, 2 * rank)), r_ref, at, y_ref.shape[1]).astype(
        BF16
    )


def z_of(ya_ref, yb_ref, r_ref, at, z_ref, first, old_ref):
    tile = z_ref.shape[2]
    users = ya_ref.shape[1]
    y = (ya_ref[...].astype(F32) + yb_ref[...].astype(F32)).astype(BF16)
    wide = math.gcd(z_ref.shape[0], 8)
    for i in range(0, z_ref.shape[0], wide):
        z = lax.dot_general(
            y,
            r_ref[at : at + users, (first + i) * tile : (first + i + wide) * tile],
            NN,
            preferred_element_type=F32,
        )
        for j in range(wide):
            part = z[:, j * tile : (j + 1) * tile]
            if old_ref is not None:
                part = part + old_ref[first + i + j]
            z_ref[i + j] = part.astype(z_ref.dtype)


def z_first_kernel(ya_ref, yb_ref, r_ref, z_ref):
    z_of(ya_ref, yb_ref, r_ref, 0, z_ref, 0, None)


def z_second_kernel(first, ya_ref, yb_ref, r_ref, old_ref, z_ref):
    z_of(ya_ref, yb_ref, r_ref, ya_ref.shape[1], z_ref, first, old_ref)


def gram_kernel(z_ref, g_ref):
    z = cat_tiles(z_ref, slice(None))
    g_ref[...] = lax.dot_general(z, z, NT, preferred_element_type=F32)


def grams_kernel(old_ref, z_ref, g_ref):
    z = cat_tiles(z_ref, slice(None))
    old = cat_tiles(old_ref, slice(None))
    both = jnp.concatenate([z, old], axis=0)
    g_ref[...] = lax.dot_general(both, z, NT, preferred_element_type=F32)


def chol_inverse(grams):
    rank = grams[0].shape[0]
    wide = 8
    blocks = rank // wide
    rows = lax.broadcasted_iota(jnp.int32, (wide, 2 * rank), 0)
    lanes = lax.broadcasted_iota(jnp.int32, (wide, 2 * rank), 1)
    mats = []
    for g in grams:
        padded = jnp.concatenate([g, jnp.zeros_like(g)], axis=1)
        mats.append(
            [
                jnp.where(lanes == rows + (rank + i * wide), 1.0, padded[i * wide : (i + 1) * wide])
                for i in range(blocks)
            ]
        )
    for p in range(blocks):
        below = range(p, blocks)
        cols = [
            [
                {
                    i: jnp.broadcast_to(
                        mat[i][:, p * wide + k : p * wide + k + 1], (wide, 2 * rank)
                    )
                    for i in below
                }
                for k in range(wide)
            ]
            for mat in mats
        ]
        for k in range(0, wide, 2):
            for mat, col in zip(mats, cols):
                d = col[k][p][k : k + 1, :]
                e = col[k][p][k + 1 : k + 2, :]
                f = col[k + 1][p][k + 1 : k + 2, :]
                first = 1.0 / d
                second = d / (d * f - e * e)
                ratio = e * first
                row = mat[p][k : k + 1, :] * first
                next_row = mat[p][k + 1 : k + 2, :] - mat[p][k : k + 1, :] * ratio
                next_scaled = next_row * second
                one, two = {}, {}
                for i in below:
                    one[i] = col[k][i]
                    two[i] = col[k + 1][i] - col[k][i] * ratio
                    if i == p:
                        one[i] = jnp.where(rows > k, one[i], 0.0)
                        two[i] = jnp.where(rows > k + 1, two[i], 0.0)
                heads = {}
                for q in range(k + 2, wide):
                    top = col[q][p][k : k + 1, :]
                    heads[q] = (
                        top * first,
                        (col[q][p][k + 1 : k + 2, :] - top * ratio) * second,
                    )
                for i in below:
                    mat[i] = mat[i] - one[i] * row - two[i] * next_scaled
                    for q in range(k + 2, wide):
                        col[q][i] = col[q][i] - one[i] * heads[q][0] - two[i] * heads[q][1]
    result = []
    for mat in mats:
        out = []
        for i in range(blocks):
            diagonal = jnp.sum(
                jnp.where(lanes == rows + i * wide, mat[i], 0.0), axis=1, keepdims=True
            )
            out.append(mat[i][:, rank:] * lax.rsqrt(diagonal))
        result.append(jnp.concatenate(out, axis=0))
    return result


def two_parts(mat):
    high = mat.astype(BF16)
    return high, (mat - high.astype(F32)).astype(BF16)


def apply_inverse(inverse, mat):
    high, low = two_parts(inverse)
    return lax.dot_general(
        jnp.concatenate([high, low], axis=1),
        jnp.concatenate([mat, mat], axis=0),
        NN,
        preferred_element_type=F32,
    )


def apply_wide(inverse, mat):
    high, low = two_parts(inverse)
    part, rest = two_parts(mat)
    return lax.dot_general(
        jnp.concatenate([high, low, high], axis=1),
        jnp.concatenate([part, part, rest], axis=0),
        NN,
        preferred_element_type=F32,
    )


def y_kernel(z_ref, r_ref, y_ref):
    y_ref[...] = y_of(cat_tiles(z_ref, slice(None)), r_ref, 0, y_ref.shape[1])


def scale_kernel(ga_ref, gb_ref, y_ref, inv_ref, out_ref):
    (inverse,) = chol_inverse([ga_ref[...] + gb_ref[...]])
    inv_ref[...] = inverse
    out_ref[...] = apply_wide(inverse, y_ref[...]).astype(BF16)


def y_scaled_kernel(at, inv_ref, z_ref, r_ref, out_ref):
    y = y_of(cat_tiles(z_ref, slice(None)), r_ref, at, out_ref.shape[1])
    out_ref[...] = apply_wide(inv_ref[...], y).astype(BF16)


def last_kernel(
    radius,
    user_scale,
    item_scale,
    slot_any,
    ga_ref,
    gb_ref,
    inv_ref,
    z_ref,
    share_ref,
    ya_0,
    ya_1,
    yb_0,
    yb_1,
    vals_ref,
    at_ref,
    bq_ref,
    user_ref,
    item_ref,
    loss_ref,
    left,
    right,
    slot_ref,
    slot_sem,
):
    slot_copy = pltpu.make_async_copy(slot_any, slot_ref, slot_sem)
    slot_copy.start()
    ya_refs, yb_refs = (ya_0, ya_1), (yb_0, yb_1)
    tile = vals_ref.shape[1]
    rank = z_ref.shape[1]
    gram = ga_ref[...] + gb_ref[...]
    y_gram = lax.dot_general(
        inv_ref[...], gram[rank:], NN, precision=lax.Precision.HIGHEST, preferred_element_type=F32
    )
    z_inv, y_inv = chol_inverse([gram[:rank], y_gram])
    for t in range(z_ref.shape[0]):
        q = apply_inverse(z_inv, z_ref[t]).astype(BF16)
        right[t, :rank] = bq_ref[t, :rank, :]
        right[t, rank : 2 * rank] = q
        right[t, 2 * rank : 3 * rank] = q
    tiles = ya_refs[0].shape[1] // tile
    for t in range(user_ref.shape[1] // tile):
        cols = slice(t * tile, (t + 1) * tile)
        here = slice(t % tiles * tile, (t % tiles + 1) * tile)
        y = ya_refs[t // tiles][:, here].astype(F32) + yb_refs[t // tiles][:, here].astype(F32)
        y_hat = apply_wide(y_inv, y)
        user_ref[:, cols] = y_hat * user_scale
        y_hat = y_hat.astype(BF16).astype(F32)
        turned = (y_hat * (-0.5 * radius)).T
        high, low = two_parts(turned)
        half = at_ref[cols, :].astype(F32) * 0.5
        left[cols, :] = jnp.concatenate([half.astype(BF16), high, low], axis=1)
    item_ref[...] = apply_wide(z_inv, share_ref[...]) * item_scale
    loss_ref[...] = jnp.zeros_like(loss_ref)
    slot_copy.wait()
    count = slot_ref[2, 0]
    many = math.gcd(vals_ref.shape[0], 64)
    few = math.gcd(many, 8)
    place = lax.broadcasted_iota(jnp.int32, (few, tile), 0)

    def losses(start, slots):
        for g in range(0, slots, few):
            at = pl.multiple_of(start + g, few)
            sums = []
            for j in range(few):
                slot = at + j
                row = pl.multiple_of(slot_ref[0, slot] * tile, tile)
                fresh = lax.dot_general(
                    left[pl.ds(row, tile), :],
                    right[slot_ref[1, slot]],
                    NN,
                    preferred_element_type=F32,
                )
                fresh = fresh - vals_ref[slot].astype(F32)
                sums.append(jnp.sum(fresh * fresh, axis=-1))
            total = jnp.where(place + at < count, jnp.stack(sums, axis=0), 0.0)
            loss_ref[pl.ds(at, few), :] = total * (1.0 / tile)

    def loop(start, stop, slots):
        def body(i, carry):
            losses(start + i * slots, slots)
            return carry

        return lax.fori_loop(0, (stop - start) // slots, body, 0)

    whole = count // many * many
    some = math.gcd(many, 16)
    loop(0, whole, many)
    loop(whole, (count + some - 1) // some * some, some)


def shards(tile_vals, tile_row, tile_col, tile_count, fac_a, fac_b, omega):
    ratings = tile_vals[0, 0]
    cap, tile, _ = ratings.shape
    rank, users_dev = fac_a.shape
    share = fac_b.shape[1]
    n_user = lax.axis_size("user")
    n_item = lax.axis_size("item")
    items_dev = share * n_user
    item_tiles = items_dev // tile
    users, items = users_dev * n_user, items_dev * n_item
    radius = math.sqrt(users * items / rank)
    me = lax.axis_index("user").astype(jnp.int32)

    by_tile = share == tile
    if not by_tile:
        order = position_of(jnp.arange(n_user, dtype=jnp.int32) ^ me, n_user)

    def to_tiles(blocks):
        if by_tile:
            return blocks
        blocks = blocks[order]
        wide = blocks.transpose(1, 0, 2).reshape(blocks.shape[1], item_tiles, tile)
        return wide.transpose(1, 0, 2)

    def to_blocks(tiles):
        if by_tile:
            return tiles
        wide = tiles.transpose(1, 0, 2).reshape(tiles.shape[1], n_user, share)
        return jnp.zeros((n_user, tiles.shape[1], share), tiles.dtype).at[order].set(
            wide.transpose(1, 0, 2)
        )

    def across(mine):
        bit = 1
        while True:
            other = lax.ppermute(mine, "item", xor_pairs(n_item, bit))
            bit *= 2
            if bit >= n_item:
                return mine, other
            mine = (mine.astype(F32) + other.astype(F32)).astype(mine.dtype)

    def reduced(near, far):
        if not by_tile:
            near, far = jnp.split(to_blocks(jnp.concatenate([near, far.astype(F32)])), 2)
        total = reduce_blocks(near, far, "user", n_user)
        groups = bit_groups(n_user)[:-1]
        return to_tiles(gather_blocks(total.astype(BF16), "user", n_user, groups)), total[0]

    def call(kernel, outs, name, *args, smem=0, hbm=0, flops=0, vmem=16, **more):
        outs = [jax.ShapeDtypeStruct(shape, dtype) for shape, dtype in outs]
        got = pl.pallas_call(
            kernel,
            out_shape=outs,
            in_specs=[SMEM] * smem
            + [pl.BlockSpec(memory_space=pl.ANY)] * hbm
            + [VMEM] * (len(args) - smem - hbm),
            out_specs=[VMEM] * len(outs),
            compiler_params=pltpu.CompilerParams(vmem_limit_bytes=vmem << 20),
            cost_estimate=pl.CostEstimate(flops=flops, bytes_accessed=1 << 16, transcendentals=0),
            name=name,
            **more,
        )(*args)
        return got[0] if len(outs) == 1 else got

    half = users_dev // 2
    r_shape = ((users_dev, items_dev), BF16)
    y_bf16, y_f32 = ((rank, half), BF16), ((rank, half), F32)
    z_bf16, z_f32 = ((item_tiles, rank, tile), BF16), ((item_tiles, rank, tile), F32)
    half_flops = 2 * rank * half * items_dev

    work = [fac_a, tile_row, tile_col, tile_count]

    def before(number, held):
        if number == 1 - len(bit_groups(n_user)):
            held, work[:] = lax.optimization_barrier((held, list(work)))
            user_factor, rows, cols, count = work
            cols = cols[0, 0]
            if by_tile:
                cols = position_of(cols ^ me, n_user)
            slots = jnp.stack([rows[0, 0], cols, jnp.broadcast_to(count[0, 0], (cap,))])
            a_t, cleared = call(
                prepare_kernel,
                [((users_dev, rank), BF16), r_shape],
                "prepare",
                user_factor,
                flops=1 << 31,
            )
            work[:] = [a_t, slots, cleared]
        elif number == -1:
            held, work[:2] = lax.optimization_barrier((held, list(work[:2])))
        return held

    both = lax.optimization_barrier(jnp.concatenate([fac_b, omega], axis=0))
    bq = to_tiles(gather_blocks(both[None], "user", n_user, bit_groups(n_user), before))
    a_t, slots, cleared = work

    def z_both(firsts, seconds):
        z = call(z_first_kernel, [z_f32], "z_first", *firsts, resid, flops=half_flops)
        near, far = item_tiles // 2, item_tiles - item_tiles // 2
        parts = (*seconds, resid, z)
        far = call(
            functools.partial(z_second_kernel, near),
            [((far, rank, tile), BF16)],
            "z_far",
            *parts,
            flops=half_flops // 2,
        )
        near = call(
            functools.partial(z_second_kernel, 0),
            [((near, rank, tile), F32)],
            "z_near",
            *parts,
            flops=half_flops // 2,
        )
        return reduced(near, far)

    resid, y_0 = call(
        first_kernel,
        [r_shape, y_bf16],
        "resid_y",
        slots,
        ratings,
        a_t,
        bq,
        cleared,
        smem=1,
        input_output_aliases={4: 0},
    )
    firsts = across(y_0)
    y_1 = call(functools.partial(omega_kernel, half), [y_bf16], "y_omega", bq, resid, flops=half_flops)
    old, _ = z_both(firsts, across(y_1))

    gram = across(call(gram_kernel, [((rank, rank), F32)], "gram", old))
    y_0 = call(y_kernel, [y_f32], "y_first", old, resid, flops=half_flops)
    inverse, y_0 = call(scale_kernel, [((rank, rank), F32), y_bf16], "scale_y", *gram, y_0)
    firsts = across(y_0)
    y_1 = call(
        functools.partial(y_scaled_kernel, half),
        [y_bf16],
        "y_second",
        inverse,
        old,
        resid,
        flops=half_flops,
    )
    seconds = across(y_1)
    z, z_share = z_both(firsts, seconds)

    grams = across(call(grams_kernel, [((2 * rank, rank), F32)], "grams", old, z))
    user_dir, item_dir, losses = call(
        functools.partial(last_kernel, radius, math.sqrt(users), math.sqrt(items)),
        [((rank, users_dev), F32), ((rank, share), F32), ((cap, tile), F32)],
        "loss",
        slots,
        *grams,
        inverse,
        z,
        z_share,
        firsts[0],
        seconds[0],
        firsts[1],
        seconds[1],
        ratings,
        a_t,
        bq,
        hbm=1,
        scratch_shapes=[
            pltpu.VMEM((users_dev, 3 * rank), BF16),
            pltpu.VMEM((item_tiles, 3 * rank, tile), BF16),
            pltpu.SMEM((3, cap), jnp.int32),
            pltpu.SemaphoreType.DMA,
        ],
    )
    return (user_dir, item_dir, losses[None, None])


def solution(mesh):
    return jax.shard_map(
        shards,
        mesh=mesh,
        in_specs=(
            P("user", "item", None, None, None),
            P("user", "item", None),
            P("user", "item", None),
            P("user", "item"),
            P(None, "user"),
            P(None, ("item", "user")),
            P(None, ("item", "user")),
        ),
        out_specs=(P(None, "user"), P(None, ("item", "user")), P("user", "item", None, None)),
        check_vma=False,
    )
```

```python
import functools
import math

import jax
import jax.numpy as jnp
from jax import lax
from jax.experimental import pallas as pl
from jax.experimental.pallas import tpu as pltpu
from jax.sharding import PartitionSpec as P

ITERS = 2
F32 = jnp.float32
BF16 = jnp.bfloat16
VMEM = pl.BlockSpec(memory_space=pltpu.VMEM)
SMEM = pl.BlockSpec(memory_space=pltpu.SMEM)
NT = (((1,), (1,)), ((), ()))
NN = (((1,), (0,)), ((), ()))


def xor_pairs(size, mask):
    return [(i, i ^ mask) for i in range(size)]


def bit_groups(size):
    bits = size.bit_length() - 1
    groups, at = [], 0
    while at < bits:
        width = 1 if at < 2 else min(2, bits - at)
        groups.append((at, width))
        at += width
    return groups


def position_of(index, size):
    place = index * 0
    for at, width in bit_groups(size):
        place = place * (1 << width) + ((index >> at) & ((1 << width) - 1))
    return place


def gather_blocks(held, axis, size, groups, before=None):
    for number, (at, width) in enumerate(reversed(groups)):
        if before is not None:
            held = before(number - len(groups), held)
        got = [held]
        for k in range(1, 1 << width):
            got.append(lax.ppermute(held, axis, xor_pairs(size, k << at)))
        held = jnp.concatenate(got, axis=0)
    return held


def reduce_blocks(near, far, axis, size, kind):
    groups = bit_groups(size)
    other = lax.ppermute(far.astype(kind), axis, xor_pairs(size, 1))
    parts = near.astype(F32) + other.astype(F32)
    for at, width in groups[1:-1]:
        ways = 1 << width
        pieces = parts.reshape((ways, parts.shape[0] // ways) + parts.shape[1:])
        total = pieces[0].astype(F32)
        got = [
            lax.ppermute(pieces[k].astype(kind), axis, xor_pairs(size, k << at))
            for k in range(1, ways)
        ]
        for piece in got:
            total = total + piece.astype(F32)
        parts = total
    at, width = groups[-1]
    mine = parts.astype(kind)
    total = mine.astype(F32)
    got = [lax.ppermute(mine, axis, xor_pairs(size, k << at)) for k in range(1, 1 << width)]
    for k, piece in enumerate(got, 1):
        total = total + jnp.stack([piece[j ^ k] for j in range(1 << width)]).astype(F32)
    return total


def y_of(q_cat, r_ref, at, users):
    return lax.dot_general(
        q_cat, r_ref[at : at + users, :], NT, preferred_element_type=F32
    )


def cat_tiles(ref, rows):
    return jnp.concatenate([ref[t, rows, :] for t in range(ref.shape[0])], axis=1)


def prepare_kernel(a_ref, at_ref, r_ref):
    tile = 128

    def clear(i, carry):
        r_ref[pl.ds(pl.multiple_of(i * tile, tile), tile), :] = jnp.zeros(
            (tile, r_ref.shape[1]), BF16
        )
        return carry

    lax.fori_loop(0, r_ref.shape[0] // tile, clear, 0)
    for t in range(at_ref.shape[0] // tile):
        cols = slice(t * tile, (t + 1) * tile)
        at_ref[cols, :] = a_ref[:, cols].astype(F32).T.astype(BF16)


def first_kernel(slot_ref, vals_ref, at_ref, bq_ref, _, r_ref, y_ref):
    tile = vals_ref.shape[1]
    rank = bq_ref.shape[1] // 2
    count = slot_ref[2, 0]
    group = math.gcd(vals_ref.shape[0], 32)

    def body(i, carry):
        for j in range(group):
            slot = i * group + j
            row = pl.multiple_of(slot_ref[0, slot] * tile, tile)
            pos = slot_ref[1, slot]
            pred = lax.dot_general(
                at_ref[pl.ds(row, tile), :],
                bq_ref[pos, :rank, :],
                NN,
                preferred_element_type=F32,
            )
            kept = jnp.where(slot < count, 1.0, 0.0)
            resid = (pred - vals_ref[slot].astype(F32)) * kept
            r_ref[pl.ds(row, tile), pl.ds(pl.multiple_of(pos * tile, tile), tile)] = resid.astype(
                BF16
            )
        return carry

    lax.fori_loop(0, (count + group - 1) // group, body, 0)
    y_ref[...] = y_of(cat_tiles(bq_ref, slice(rank, 2 * rank)), r_ref, 0, y_ref.shape[1])


def omega_kernel(at, bq_ref, r_ref, y_ref):
    rank = bq_ref.shape[1] // 2
    y_ref[...] = y_of(cat_tiles(bq_ref, slice(rank, 2 * rank)), r_ref, at, y_ref.shape[1])


def z_of(y, r_ref, at, z_ref, first, old_ref):
    tile = z_ref.shape[2]
    users = y.shape[1]
    wide = math.gcd(z_ref.shape[0], 8)
    for i in range(0, z_ref.shape[0], wide):
        z = lax.dot_general(
            y,
            r_ref[at : at + users, (first + i) * tile : (first + i + wide) * tile],
            NN,
            preferred_element_type=F32,
        )
        for j in range(wide):
            part = z[:, j * tile : (j + 1) * tile]
            if old_ref is not None:
                part = part + old_ref[first + i + j]
            z_ref[i + j] = part.astype(z_ref.dtype)


def exact_dot(left, right, dims):
    return lax.dot_general(
        left, right, dims, precision=lax.Precision.HIGHEST, preferred_element_type=F32
    )


def y_gram_kernel(ya_ref, yb_ref, y_ref, g_ref):
    y = ya_ref[...] + yb_ref[...]
    y_ref[...] = y
    g_ref[...] = exact_dot(y, y, NT)


def y_gram_more_kernel(ya_ref, yb_ref, old_ref, y_ref, g_ref):
    y = ya_ref[...] + yb_ref[...]
    y_ref[...] = y
    g_ref[...] = old_ref[...] + exact_dot(y, y, NT)


def y_hat_kernel(g_ref, y_0, y_1, out_ref):
    (inverse,) = chol_inverse([g_ref[...]])
    half = y_0.shape[1]
    out_ref[:, :half] = apply_wide(inverse, y_0[...])
    out_ref[:, half:] = apply_wide(inverse, y_1[...])


def y_near_hat_kernel(g_ref, y_0, ya_ref, yb_ref, out_ref):
    gram = g_ref[...]
    rows = lax.broadcasted_iota(jnp.int32, gram.shape, 0)
    diagonal = rows == lax.broadcasted_iota(jnp.int32, gram.shape, 1)
    (inverse,) = chol_inverse([gram + jnp.where(diagonal, gram * 1e-6 + 1e-30, 0.0)])
    half = y_0.shape[1]
    out_ref[:, :half] = apply_wide(inverse, y_0[...])
    out_ref[:, half:] = apply_wide(inverse, ya_ref[...] + yb_ref[...])


def z_kernel(first, y_ref, r_ref, z_ref):
    z_of(y_ref[...].astype(BF16), r_ref, 0, z_ref, first, None)


def gram_kernel(z_ref, g_ref):
    z = cat_tiles(z_ref, slice(None))
    if z.dtype == F32:
        g_ref[...] = exact_dot(z, z, NT)
    else:
        g_ref[...] = lax.dot_general(z, z, NT, preferred_element_type=F32)


def chol_inverse(grams):
    rank = grams[0].shape[0]
    wide = 8
    blocks = rank // wide
    rows = lax.broadcasted_iota(jnp.int32, (wide, 2 * rank), 0)
    lanes = lax.broadcasted_iota(jnp.int32, (wide, 2 * rank), 1)
    mats = []
    for g in grams:
        padded = jnp.concatenate([g, jnp.zeros_like(g)], axis=1)
        mats.append(
            [
                jnp.where(lanes == rows + (rank + i * wide), 1.0, padded[i * wide : (i + 1) * wide])
                for i in range(blocks)
            ]
        )
    for p in range(blocks):
        below = range(p, blocks)
        cols = [
            [
                {
                    i: jnp.broadcast_to(
                        mat[i][:, p * wide + k : p * wide + k + 1], (wide, 2 * rank)
                    )
                    for i in below
                }
                for k in range(wide)
            ]
            for mat in mats
        ]
        for k in range(0, wide, 2):
            for mat, col in zip(mats, cols):
                d = col[k][p][k : k + 1, :]
                e = col[k][p][k + 1 : k + 2, :]
                f = col[k + 1][p][k + 1 : k + 2, :]
                first = 1.0 / d
                second = d / (d * f - e * e)
                ratio = e * first
                row = mat[p][k : k + 1, :] * first
                next_row = mat[p][k + 1 : k + 2, :] - mat[p][k : k + 1, :] * ratio
                next_scaled = next_row * second
                one, two = {}, {}
                for i in below:
                    one[i] = col[k][i]
                    two[i] = col[k + 1][i] - col[k][i] * ratio
                    if i == p:
                        one[i] = jnp.where(rows > k, one[i], 0.0)
                        two[i] = jnp.where(rows > k + 1, two[i], 0.0)
                heads = {}
                for q in range(k + 2, wide):
                    top = col[q][p][k : k + 1, :]
                    heads[q] = (
                        top * first,
                        (col[q][p][k + 1 : k + 2, :] - top * ratio) * second,
                    )
                for i in below:
                    mat[i] = mat[i] - one[i] * row - two[i] * next_scaled
                    for q in range(k + 2, wide):
                        col[q][i] = col[q][i] - one[i] * heads[q][0] - two[i] * heads[q][1]
    result = []
    for mat in mats:
        out = []
        for i in range(blocks):
            diagonal = jnp.sum(
                jnp.where(lanes == rows + i * wide, mat[i], 0.0), axis=1, keepdims=True
            )
            out.append(mat[i][:, rank:] * lax.rsqrt(diagonal))
        result.append(jnp.concatenate(out, axis=0))
    return result


def two_parts(mat):
    high = mat.astype(BF16)
    return high, (mat - high.astype(F32)).astype(BF16)


def apply_inverse(inverse, mat):
    high, low = two_parts(inverse)
    return lax.dot_general(
        jnp.concatenate([high, low], axis=1),
        jnp.concatenate([mat, mat], axis=0),
        NN,
        preferred_element_type=F32,
    )


def apply_wide(inverse, mat):
    high, low = two_parts(inverse)
    part, rest = two_parts(mat)
    return lax.dot_general(
        jnp.concatenate([high, low, high], axis=1),
        jnp.concatenate([part, part, rest], axis=0),
        NN,
        preferred_element_type=F32,
    )


def q_kernel(ga_ref, gb_ref, z_ref, q_ref):
    (inverse,) = chol_inverse([ga_ref[...] + gb_ref[...]])
    for t in range(z_ref.shape[0]):
        q_ref[t] = apply_wide(inverse, z_ref[t]).astype(BF16)


def y_kernel(at, q_ref, r_ref, y_ref):
    y_ref[...] = y_of(cat_tiles(q_ref, slice(None)), r_ref, at, y_ref.shape[1])


def left_kernel(radius, user_scale, y_ref, at_ref, left_ref, user_ref):
    tile = 128
    user_ref[...] = y_ref[...] * user_scale
    for t in range(0, y_ref.shape[1], tile):
        rows = slice(t, t + tile)
        turned = (y_ref[:, rows].astype(BF16).astype(F32) * (-0.5 * radius)).T
        high, low = two_parts(turned)
        half = at_ref[rows, :].astype(F32) * 0.5
        left_ref[rows, :] = jnp.concatenate([half.astype(BF16), high, low], axis=1)


def last_kernel(
    item_scale,
    slot_any,
    ga_ref,
    gb_ref,
    z_ref,
    share_ref,
    vals_ref,
    left,
    bq_ref,
    item_ref,
    loss_ref,
    right,
    slot_ref,
    slot_sem,
):
    slot_copy = pltpu.make_async_copy(slot_any, slot_ref, slot_sem)
    slot_copy.start()
    tile = vals_ref.shape[1]
    rank = z_ref.shape[1]
    (z_inv,) = chol_inverse([ga_ref[...] + gb_ref[...]])
    for t in range(z_ref.shape[0]):
        q = apply_inverse(z_inv, z_ref[t]).astype(BF16)
        right[t, :rank] = bq_ref[t, :rank, :]
        right[t, rank : 2 * rank] = q
        right[t, 2 * rank : 3 * rank] = q
    item_ref[...] = apply_wide(z_inv, share_ref[...]) * item_scale
    loss_ref[...] = jnp.zeros_like(loss_ref)
    slot_copy.wait()
    count = slot_ref[2, 0]
    many = math.gcd(vals_ref.shape[0], 64)
    few = math.gcd(many, 8)
    place = lax.broadcasted_iota(jnp.int32, (few, tile), 0)

    def losses(start, slots):
        for g in range(0, slots, few):
            at = pl.multiple_of(start + g, few)
            sums = []
            for j in range(few):
                slot = at + j
                row = pl.multiple_of(slot_ref[0, slot] * tile, tile)
                fresh = lax.dot_general(
                    left[pl.ds(row, tile), :],
                    right[slot_ref[1, slot]],
                    NN,
                    preferred_element_type=F32,
                )
                fresh = fresh - vals_ref[slot].astype(F32)
                sums.append(jnp.sum(fresh * fresh, axis=-1))
            total = jnp.where(place + at < count, jnp.stack(sums, axis=0), 0.0)
            loss_ref[pl.ds(at, few), :] = total * (1.0 / tile)

    def loop(start, stop, slots):
        def body(i, carry):
            losses(start + i * slots, slots)
            return carry

        return lax.fori_loop(0, (stop - start) // slots, body, 0)

    whole = count // many * many
    some = math.gcd(many, 16)
    loop(0, whole, many)
    loop(whole, (count + some - 1) // some * some, some)


def shards(tile_vals, tile_row, tile_col, tile_count, fac_a, fac_b, omega):
    ratings = tile_vals[0, 0]
    cap, tile, _ = ratings.shape
    rank, users_dev = fac_a.shape
    share = fac_b.shape[1]
    n_user = lax.axis_size("user")
    n_item = lax.axis_size("item")
    items_dev = share * n_user
    item_tiles = items_dev // tile
    users, items = users_dev * n_user, items_dev * n_item
    radius = math.sqrt(users * items / rank)
    me = lax.axis_index("user").astype(jnp.int32)

    by_tile = share == tile
    if not by_tile:
        order = position_of(jnp.arange(n_user, dtype=jnp.int32) ^ me, n_user)

    def to_tiles(blocks):
        if by_tile:
            return blocks
        blocks = blocks[order]
        wide = blocks.transpose(1, 0, 2).reshape(blocks.shape[1], item_tiles, tile)
        return wide.transpose(1, 0, 2)

    def to_blocks(tiles):
        if by_tile:
            return tiles
        wide = tiles.transpose(1, 0, 2).reshape(tiles.shape[1], n_user, share)
        return jnp.zeros((n_user, tiles.shape[1], share), tiles.dtype).at[order].set(
            wide.transpose(1, 0, 2)
        )

    def across(mine):
        bit = 1
        while True:
            other = lax.ppermute(mine, "item", xor_pairs(n_item, bit))
            bit *= 2
            if bit >= n_item:
                return mine, other
            mine = (mine.astype(F32) + other.astype(F32)).astype(mine.dtype)

    def reduced(near, far, kind, work=()):
        if not by_tile:
            near, far = jnp.split(to_blocks(jnp.concatenate([near, far.astype(F32)])), 2)
        total = reduce_blocks(near, far, "user", n_user, kind)
        work = list(work)

        def before(number, held):
            if number == -1 and work:
                held, work[:] = lax.optimization_barrier((held, list(work)))
            return held

        groups = bit_groups(n_user)[:-1]
        z = gather_blocks(total.astype(kind), "user", n_user, groups, before)
        return to_tiles(z), total[0], work

    def call(kernel, outs, name, *args, smem=0, hbm=0, flops=0, vmem=16, **more):
        outs = [jax.ShapeDtypeStruct(shape, dtype) for shape, dtype in outs]
        got = pl.pallas_call(
            kernel,
            out_shape=outs,
            in_specs=[SMEM] * smem
            + [pl.BlockSpec(memory_space=pl.ANY)] * hbm
            + [VMEM] * (len(args) - smem - hbm),
            out_specs=[VMEM] * len(outs),
            compiler_params=pltpu.CompilerParams(vmem_limit_bytes=vmem << 20),
            cost_estimate=pl.CostEstimate(flops=flops, bytes_accessed=1 << 16, transcendentals=0),
            name=name,
            **more,
        )(*args)
        return got[0] if len(outs) == 1 else got

    half = users_dev // 2
    r_shape = ((users_dev, items_dev), BF16)
    y_f32 = ((rank, half), F32)
    half_flops = 2 * rank * half * items_dev

    work = [fac_a, tile_row, tile_col, tile_count]

    def before(number, held):
        if number == 1 - len(bit_groups(n_user)):
            held, work[:] = lax.optimization_barrier((held, list(work)))
            user_factor, rows, cols, count = work
            cols = cols[0, 0]
            if by_tile:
                cols = position_of(cols ^ me, n_user)
            slots = jnp.stack([rows[0, 0], cols, jnp.broadcast_to(count[0, 0], (cap,))])
            a_t, cleared = call(
                prepare_kernel,
                [((users_dev, rank), BF16), r_shape],
                "prepare",
                user_factor,
                flops=1 << 31,
            )
            work[:] = [a_t, slots, cleared]
        elif number == -1:
            held, work[:2] = lax.optimization_barrier((held, list(work[:2])))
        return held

    both = lax.optimization_barrier(jnp.concatenate([fac_b, omega], axis=0))
    bq = to_tiles(gather_blocks(both[None], "user", n_user, bit_groups(n_user), before))
    a_t, slots, cleared = work

    def over_users(part):
        for at, width in bit_groups(n_user):
            terms = [part]
            for k in range(1, 1 << width):
                terms.append(lax.ppermute(part, "user", xor_pairs(n_user, k << at)))
            while len(terms) > 1:
                terms = [a + b for a, b in zip(terms[::2], terms[1::2])]
            part = terms[0]
        return part

    square = ((rank, rank), F32)

    def user_step(firsts, seconds, exact):
        y_0, gram = call(y_gram_kernel, [y_f32, square], "y_gram", *firsts, flops=half_flops)
        whole = [((rank, users_dev), F32)]
        if not exact:
            return call(y_near_hat_kernel, whole, "y_hat", over_users(gram), y_0, *seconds)
        y_1, gram = call(y_gram_more_kernel, [y_f32, square], "y_gram_more", *seconds, gram)
        return call(y_hat_kernel, whole, "y_hat", over_users(gram), y_0, y_1)

    def item_step(y_hat, kind, work=()):
        near, far = item_tiles // 2, item_tiles - item_tiles // 2
        kernel = functools.partial(z_kernel, near)
        later = call(
            kernel, [((far, rank, tile), kind)], "z_far", y_hat, resid, flops=half_flops
        )
        kernel = functools.partial(z_kernel, 0)
        sooner = call(
            kernel, [((near, rank, tile), F32)], "z_near", y_hat, resid, flops=half_flops
        )
        return reduced(sooner, later, kind, work)

    resid, y_0 = call(
        first_kernel,
        [r_shape, y_f32],
        "resid_y",
        slots,
        ratings,
        a_t,
        bq,
        cleared,
        smem=1,
        input_output_aliases={4: 0},
    )
    firsts = across(y_0)
    y_1 = call(functools.partial(omega_kernel, half), [y_f32], "y_omega", bq, resid, flops=half_flops)
    seconds = across(y_1)
    old, _, _ = item_step(user_step(firsts, seconds, False), F32)

    gram = across(call(gram_kernel, [square], "gram", old))
    q = call(q_kernel, [((item_tiles, rank, tile), BF16)], "q", *gram, old)
    kernel = functools.partial(y_kernel, 0)
    firsts = across(call(kernel, [y_f32], "y_first", q, resid, flops=half_flops))
    kernel = functools.partial(y_kernel, half)
    seconds = across(call(kernel, [y_f32], "y_second", q, resid, flops=half_flops))
    y_hat = user_step(firsts, seconds, True)
    left, user_dir = call(
        functools.partial(left_kernel, radius, math.sqrt(users)),
        [((users_dev, 3 * rank), BF16), ((rank, users_dev), F32)],
        "left",
        y_hat,
        a_t,
        flops=1 << 30,
    )
    z, z_share, (left, user_dir) = item_step(y_hat, BF16, (left, user_dir))

    grams = across(call(gram_kernel, [square], "gram", z))
    item_dir, losses = call(
        functools.partial(last_kernel, math.sqrt(items)),
        [((rank, share), F32), ((cap, tile), F32)],
        "loss",
        slots,
        *grams,
        z,
        z_share,
        ratings,
        left,
        bq,
        hbm=1,
        scratch_shapes=[
            pltpu.VMEM((item_tiles, 3 * rank, tile), BF16),
            pltpu.SMEM((3, cap), jnp.int32),
            pltpu.SemaphoreType.DMA,
        ],
    )
    return (user_dir, item_dir, losses[None, None])


def solution(mesh):
    return jax.shard_map(
        shards,
        mesh=mesh,
        in_specs=(
            P("user", "item", None, None, None),
            P("user", "item", None),
            P("user", "item", None),
            P("user", "item"),
            P(None, "user"),
            P(None, ("item", "user")),
            P(None, ("item", "user")),
        ),
        out_specs=(P(None, "user"), P(None, ("item", "user")), P("user", "item", None, None)),
        check_vma=False,
    )
```

```python
import functools
import math

import jax
import jax.numpy as jnp
from jax import lax
from jax.experimental import pallas as pl
from jax.experimental.pallas import tpu as pltpu
from jax.sharding import PartitionSpec as P

ITERS = 2
F32 = jnp.float32
BF16 = jnp.bfloat16
VMEM = pl.BlockSpec(memory_space=pltpu.VMEM)
SMEM = pl.BlockSpec(memory_space=pltpu.SMEM)
NT = (((1,), (1,)), ((), ()))
NN = (((1,), (0,)), ((), ()))


def xor_pairs(size, mask):
    return [(i, i ^ mask) for i in range(size)]


def bit_groups(size):
    bits = size.bit_length() - 1
    groups, at = [], 0
    while at < bits:
        width = 1 if at < 2 else min(2, bits - at)
        groups.append((at, width))
        at += width
    return groups


def position_of(index, size):
    place = index * 0
    for at, width in bit_groups(size):
        place = place * (1 << width) + ((index >> at) & ((1 << width) - 1))
    return place


def gather_blocks(held, axis, size, groups, before=None):
    for number, (at, width) in enumerate(reversed(groups)):
        if before is not None:
            held = before(number - len(groups), held)
        got = [held]
        for k in range(1, 1 << width):
            got.append(lax.ppermute(held, axis, xor_pairs(size, k << at)))
        held = jnp.concatenate(got, axis=0)
    return held


def reduce_blocks(near, far, axis, size, kind):
    groups = bit_groups(size)
    other = lax.ppermute(far.astype(kind), axis, xor_pairs(size, 1))
    parts = near.astype(F32) + other.astype(F32)
    for at, width in groups[1:-1]:
        ways = 1 << width
        pieces = parts.reshape((ways, parts.shape[0] // ways) + parts.shape[1:])
        total = pieces[0].astype(F32)
        got = [
            lax.ppermute(pieces[k].astype(kind), axis, xor_pairs(size, k << at))
            for k in range(1, ways)
        ]
        for piece in got:
            total = total + piece.astype(F32)
        parts = total
    at, width = groups[-1]
    mine = parts.astype(kind)
    total = mine.astype(F32)
    got = [lax.ppermute(mine, axis, xor_pairs(size, k << at)) for k in range(1, 1 << width)]
    for k, piece in enumerate(got, 1):
        total = total + jnp.stack([piece[j ^ k] for j in range(1 << width)]).astype(F32)
    return total


def y_of(q_cat, r_ref, at, users):
    return lax.dot_general(
        q_cat, r_ref[at : at + users, :], NT, preferred_element_type=F32
    )


def cat_tiles(ref, rows):
    return jnp.concatenate([ref[t, rows, :] for t in range(ref.shape[0])], axis=1)


def prepare_kernel(a_ref, at_ref, r_ref):
    tile = 128

    def clear(i, carry):
        r_ref[pl.ds(pl.multiple_of(i * tile, tile), tile), :] = jnp.zeros(
            (tile, r_ref.shape[1]), BF16
        )
        return carry

    lax.fori_loop(0, r_ref.shape[0] // tile, clear, 0)
    for t in range(at_ref.shape[0] // tile):
        cols = slice(t * tile, (t + 1) * tile)
        at_ref[cols, :] = a_ref[:, cols].astype(F32).T.astype(BF16)


def first_kernel(slot_ref, vals_ref, at_ref, bq_ref, _, r_ref, y_ref):
    tile = vals_ref.shape[1]
    rank = bq_ref.shape[1] // 2
    count = slot_ref[2, 0]
    group = math.gcd(vals_ref.shape[0], 32)

    def body(i, carry):
        for j in range(group):
            slot = i * group + j
            row = pl.multiple_of(slot_ref[0, slot] * tile, tile)
            pos = slot_ref[1, slot]
            pred = lax.dot_general(
                at_ref[pl.ds(row, tile), :],
                bq_ref[pos, :rank, :],
                NN,
                preferred_element_type=F32,
            )
            kept = jnp.where(slot < count, 1.0, 0.0)
            resid = (pred - vals_ref[slot].astype(F32)) * kept
            r_ref[pl.ds(row, tile), pl.ds(pl.multiple_of(pos * tile, tile), tile)] = resid.astype(
                BF16
            )
        return carry

    lax.fori_loop(0, (count + group - 1) // group, body, 0)
    y_ref[...] = y_of(cat_tiles(bq_ref, slice(rank, 2 * rank)), r_ref, 0, y_ref.shape[1])


def omega_kernel(at, bq_ref, r_ref, y_ref):
    rank = bq_ref.shape[1] // 2
    y_ref[...] = y_of(cat_tiles(bq_ref, slice(rank, 2 * rank)), r_ref, at, y_ref.shape[1])


def z_of(y, r_ref, at, z_ref, first, old_ref):
    tile = z_ref.shape[2]
    users = y.shape[1]
    wide = math.gcd(z_ref.shape[0], 8)
    for i in range(0, z_ref.shape[0], wide):
        z = lax.dot_general(
            y,
            r_ref[at : at + users, (first + i) * tile : (first + i + wide) * tile],
            NN,
            preferred_element_type=F32,
        )
        for j in range(wide):
            part = z[:, j * tile : (j + 1) * tile]
            if old_ref is not None:
                part = part + old_ref[first + i + j]
            z_ref[i + j] = part.astype(z_ref.dtype)


def exact_dot(left, right, dims):
    return lax.dot_general(
        left, right, dims, precision=lax.Precision.HIGHEST, preferred_element_type=F32
    )


def y_gram_kernel(ya_ref, yb_ref, y_ref, g_ref):
    y = ya_ref[...].astype(F32) + yb_ref[...].astype(F32)
    y_ref[...] = y
    g_ref[...] = exact_dot(y, y, NT)


def y_gram_more_kernel(ya_ref, yb_ref, old_ref, y_ref, g_ref):
    y = ya_ref[...].astype(F32) + yb_ref[...].astype(F32)
    y_ref[...] = y
    g_ref[...] = old_ref[...] + exact_dot(y, y, NT)


def y_hat_kernel(g_ref, y_0, y_1, out_ref):
    (inverse,) = chol_inverse([g_ref[...]])
    half = y_0.shape[1]
    out_ref[:, :half] = apply_wide(inverse, y_0[...])
    out_ref[:, half:] = apply_wide(inverse, y_1[...])


def y_near_hat_kernel(g_ref, y_0, ya_ref, yb_ref, out_ref):
    gram = g_ref[...]
    rows = lax.broadcasted_iota(jnp.int32, gram.shape, 0)
    diagonal = rows == lax.broadcasted_iota(jnp.int32, gram.shape, 1)
    (inverse,) = chol_inverse([gram + jnp.where(diagonal, gram * 1e-6 + 1e-30, 0.0)])
    half = y_0.shape[1]
    out_ref[:, :half] = apply_wide(inverse, y_0[...])
    out_ref[:, half:] = apply_wide(inverse, ya_ref[...] + yb_ref[...])


def z_kernel(first, y_ref, r_ref, z_ref):
    z_of(y_ref[...].astype(BF16), r_ref, 0, z_ref, first, None)


def gram_kernel(z_ref, g_ref):
    z = cat_tiles(z_ref, slice(None))
    if z.dtype == F32:
        g_ref[...] = exact_dot(z, z, NT)
    else:
        g_ref[...] = lax.dot_general(z, z, NT, preferred_element_type=F32)


def chol_inverse(grams):
    rank = grams[0].shape[0]
    wide = 8
    blocks = rank // wide
    rows = lax.broadcasted_iota(jnp.int32, (wide, 2 * rank), 0)
    lanes = lax.broadcasted_iota(jnp.int32, (wide, 2 * rank), 1)
    mats = []
    for g in grams:
        padded = jnp.concatenate([g, jnp.zeros_like(g)], axis=1)
        mats.append(
            [
                jnp.where(lanes == rows + (rank + i * wide), 1.0, padded[i * wide : (i + 1) * wide])
                for i in range(blocks)
            ]
        )
    for p in range(blocks):
        below = range(p, blocks)
        cols = [
            [
                {
                    i: jnp.broadcast_to(
                        mat[i][:, p * wide + k : p * wide + k + 1], (wide, 2 * rank)
                    )
                    for i in below
                }
                for k in range(wide)
            ]
            for mat in mats
        ]
        for k in range(0, wide, 2):
            for mat, col in zip(mats, cols):
                d = col[k][p][k : k + 1, :]
                e = col[k][p][k + 1 : k + 2, :]
                f = col[k + 1][p][k + 1 : k + 2, :]
                first = 1.0 / d
                second = d / (d * f - e * e)
                ratio = e * first
                row = mat[p][k : k + 1, :] * first
                next_row = mat[p][k + 1 : k + 2, :] - mat[p][k : k + 1, :] * ratio
                next_scaled = next_row * second
                one, two = {}, {}
                for i in below:
                    one[i] = col[k][i]
                    two[i] = col[k + 1][i] - col[k][i] * ratio
                    if i == p:
                        one[i] = jnp.where(rows > k, one[i], 0.0)
                        two[i] = jnp.where(rows > k + 1, two[i], 0.0)
                heads = {}
                for q in range(k + 2, wide):
                    top = col[q][p][k : k + 1, :]
                    heads[q] = (
                        top * first,
                        (col[q][p][k + 1 : k + 2, :] - top * ratio) * second,
                    )
                for i in below:
                    mat[i] = mat[i] - one[i] * row - two[i] * next_scaled
                    for q in range(k + 2, wide):
                        col[q][i] = col[q][i] - one[i] * heads[q][0] - two[i] * heads[q][1]
    result = []
    for mat in mats:
        out = []
        for i in range(blocks):
            diagonal = jnp.sum(
                jnp.where(lanes == rows + i * wide, mat[i], 0.0), axis=1, keepdims=True
            )
            out.append(mat[i][:, rank:] * lax.rsqrt(diagonal))
        result.append(jnp.concatenate(out, axis=0))
    return result


def two_parts(mat):
    high = mat.astype(BF16)
    return high, (mat - high.astype(F32)).astype(BF16)


def apply_inverse(inverse, mat):
    high, low = two_parts(inverse)
    return lax.dot_general(
        jnp.concatenate([high, low], axis=1),
        jnp.concatenate([mat, mat], axis=0),
        NN,
        preferred_element_type=F32,
    )


def apply_wide(inverse, mat):
    high, low = two_parts(inverse)
    part, rest = two_parts(mat)
    return lax.dot_general(
        jnp.concatenate([high, low, high], axis=1),
        jnp.concatenate([part, part, rest], axis=0),
        NN,
        preferred_element_type=F32,
    )


def q_kernel(ga_ref, gb_ref, z_ref, q_ref):
    (inverse,) = chol_inverse([ga_ref[...] + gb_ref[...]])
    for t in range(z_ref.shape[0]):
        q_ref[t] = apply_wide(inverse, z_ref[t]).astype(BF16)


def y_kernel(at, q_ref, r_ref, y_ref):
    y = y_of(cat_tiles(q_ref, slice(None)), r_ref, at, y_ref.shape[1])
    y_ref[...] = y.astype(y_ref.dtype)


def left_kernel(radius, user_scale, y_ref, at_ref, left_ref, user_ref):
    tile = 128
    user_ref[...] = y_ref[...] * user_scale
    for t in range(0, y_ref.shape[1], tile):
        rows = slice(t, t + tile)
        turned = (y_ref[:, rows].astype(BF16).astype(F32) * (-0.5 * radius)).T
        high, low = two_parts(turned)
        half = at_ref[rows, :].astype(F32) * 0.5
        left_ref[rows, :] = jnp.concatenate([half.astype(BF16), high, low], axis=1)


def last_kernel(
    item_scale,
    slot_any,
    ga_ref,
    gb_ref,
    z_ref,
    share_ref,
    vals_ref,
    left,
    bq_ref,
    item_ref,
    loss_ref,
    right,
    slot_ref,
    slot_sem,
):
    slot_copy = pltpu.make_async_copy(slot_any, slot_ref, slot_sem)
    slot_copy.start()
    tile = vals_ref.shape[1]
    rank = z_ref.shape[1]
    (z_inv,) = chol_inverse([ga_ref[...] + gb_ref[...]])
    for t in range(z_ref.shape[0]):
        q = apply_inverse(z_inv, z_ref[t]).astype(BF16)
        right[t, :rank] = bq_ref[t, :rank, :]
        right[t, rank : 2 * rank] = q
        right[t, 2 * rank : 3 * rank] = q
    item_ref[...] = apply_wide(z_inv, share_ref[...]) * item_scale
    loss_ref[...] = jnp.zeros_like(loss_ref)
    slot_copy.wait()
    count = slot_ref[2, 0]
    many = math.gcd(vals_ref.shape[0], 64)
    few = math.gcd(many, 8)
    place = lax.broadcasted_iota(jnp.int32, (few, tile), 0)

    def losses(start, slots):
        for g in range(0, slots, few):
            at = pl.multiple_of(start + g, few)
            sums = []
            for j in range(few):
                slot = at + j
                row = pl.multiple_of(slot_ref[0, slot] * tile, tile)
                fresh = lax.dot_general(
                    left[pl.ds(row, tile), :],
                    right[slot_ref[1, slot]],
                    NN,
                    preferred_element_type=F32,
                )
                fresh = fresh - vals_ref[slot].astype(F32)
                sums.append(jnp.sum(fresh * fresh, axis=-1))
            total = jnp.where(place + at < count, jnp.stack(sums, axis=0), 0.0)
            loss_ref[pl.ds(at, few), :] = total * (1.0 / tile)

    def loop(start, stop, slots):
        def body(i, carry):
            losses(start + i * slots, slots)
            return carry

        return lax.fori_loop(0, (stop - start) // slots, body, 0)

    whole = count // many * many
    some = math.gcd(many, 16)
    loop(0, whole, many)
    loop(whole, (count + some - 1) // some * some, some)


def shards(tile_vals, tile_row, tile_col, tile_count, fac_a, fac_b, omega):
    ratings = tile_vals[0, 0]
    cap, tile, _ = ratings.shape
    rank, users_dev = fac_a.shape
    share = fac_b.shape[1]
    n_user = lax.axis_size("user")
    n_item = lax.axis_size("item")
    items_dev = share * n_user
    item_tiles = items_dev // tile
    users, items = users_dev * n_user, items_dev * n_item
    radius = math.sqrt(users * items / rank)
    me = lax.axis_index("user").astype(jnp.int32)

    by_tile = share == tile
    if not by_tile:
        order = position_of(jnp.arange(n_user, dtype=jnp.int32) ^ me, n_user)

    def to_tiles(blocks):
        if by_tile:
            return blocks
        blocks = blocks[order]
        wide = blocks.transpose(1, 0, 2).reshape(blocks.shape[1], item_tiles, tile)
        return wide.transpose(1, 0, 2)

    def to_blocks(tiles):
        if by_tile:
            return tiles
        wide = tiles.transpose(1, 0, 2).reshape(tiles.shape[1], n_user, share)
        return jnp.zeros((n_user, tiles.shape[1], share), tiles.dtype).at[order].set(
            wide.transpose(1, 0, 2)
        )

    def across(mine):
        bit = 1
        while True:
            other = lax.ppermute(mine, "item", xor_pairs(n_item, bit))
            bit *= 2
            if bit >= n_item:
                return mine, other
            mine = (mine.astype(F32) + other.astype(F32)).astype(mine.dtype)

    def reduced(near, far, kind, work=()):
        if not by_tile:
            near, far = jnp.split(to_blocks(jnp.concatenate([near, far.astype(F32)])), 2)
        total = reduce_blocks(near, far, "user", n_user, kind)
        work = list(work)

        def before(number, held):
            if number == -1 and work:
                held, work[:] = lax.optimization_barrier((held, list(work)))
            return held

        groups = bit_groups(n_user)[:-1]
        z = gather_blocks(total.astype(kind), "user", n_user, groups, before)
        return to_tiles(z), total[0], work

    def call(kernel, outs, name, *args, smem=0, hbm=0, flops=0, vmem=16, **more):
        outs = [jax.ShapeDtypeStruct(shape, dtype) for shape, dtype in outs]
        got = pl.pallas_call(
            kernel,
            out_shape=outs,
            in_specs=[SMEM] * smem
            + [pl.BlockSpec(memory_space=pl.ANY)] * hbm
            + [VMEM] * (len(args) - smem - hbm),
            out_specs=[VMEM] * len(outs),
            compiler_params=pltpu.CompilerParams(vmem_limit_bytes=vmem << 20),
            cost_estimate=pl.CostEstimate(flops=flops, bytes_accessed=1 << 16, transcendentals=0),
            name=name,
            **more,
        )(*args)
        return got[0] if len(outs) == 1 else got

    half = users_dev // 2
    r_shape = ((users_dev, items_dev), BF16)
    y_f32, y_bf16 = ((rank, half), F32), ((rank, half), BF16)
    some = users_dev // 4
    y_some, y_rest = ((rank, some), F32), ((rank, users_dev - some), F32)
    half_flops = 2 * rank * half * items_dev

    work = [fac_a, tile_row, tile_col, tile_count]

    def before(number, held):
        if number == 1 - len(bit_groups(n_user)):
            held, work[:] = lax.optimization_barrier((held, list(work)))
            user_factor, rows, cols, count = work
            cols = cols[0, 0]
            if by_tile:
                cols = position_of(cols ^ me, n_user)
            slots = jnp.stack([rows[0, 0], cols, jnp.broadcast_to(count[0, 0], (cap,))])
            a_t, cleared = call(
                prepare_kernel,
                [((users_dev, rank), BF16), r_shape],
                "prepare",
                user_factor,
                flops=1 << 31,
            )
            work[:] = [a_t, slots, cleared]
        elif number == -1:
            held, work[:2] = lax.optimization_barrier((held, list(work[:2])))
        return held

    both = lax.optimization_barrier(jnp.concatenate([fac_b, omega], axis=0))
    bq = to_tiles(gather_blocks(both[None], "user", n_user, bit_groups(n_user), before))
    a_t, slots, cleared = work

    def over_users(part):
        for at, width in bit_groups(n_user):
            terms = [part]
            for k in range(1, 1 << width):
                terms.append(lax.ppermute(part, "user", xor_pairs(n_user, k << at)))
            while len(terms) > 1:
                terms = [a + b for a, b in zip(terms[::2], terms[1::2])]
            part = terms[0]
        return part

    square = ((rank, rank), F32)

    def user_step(firsts, seconds, exact):
        summed = [(firsts[0].shape, F32), square]
        y_0, gram = call(y_gram_kernel, summed, "y_gram", *firsts, flops=half_flops)
        whole = [((rank, users_dev), F32)]
        if not exact:
            return call(y_near_hat_kernel, whole, "y_hat", over_users(gram), y_0, *seconds)
        y_1, gram = call(y_gram_more_kernel, [y_f32, square], "y_gram_more", *seconds, gram)
        return call(y_hat_kernel, whole, "y_hat", over_users(gram), y_0, y_1)

    def item_step(y_hat, kind, work=()):
        near, far = item_tiles // 2, item_tiles - item_tiles // 2
        kernel = functools.partial(z_kernel, near)
        later = call(
            kernel, [((far, rank, tile), kind)], "z_far", y_hat, resid, flops=half_flops
        )
        kernel = functools.partial(z_kernel, 0)
        sooner = call(
            kernel, [((near, rank, tile), F32)], "z_near", y_hat, resid, flops=half_flops
        )
        return reduced(sooner, later, kind, work)

    resid, y_0 = call(
        first_kernel,
        [r_shape, y_some],
        "resid_y",
        slots,
        ratings,
        a_t,
        bq,
        cleared,
        smem=1,
        input_output_aliases={4: 0},
    )
    firsts = across(y_0)
    kernel = functools.partial(omega_kernel, some)
    y_1 = call(kernel, [y_rest], "y_omega", bq, resid, flops=half_flops)
    firsts, y_1 = lax.optimization_barrier((firsts, y_1))
    seconds = across(y_1)
    old, _, _ = item_step(user_step(firsts, seconds, False), F32)

    gram = across(call(gram_kernel, [square], "gram", old))
    q = call(q_kernel, [((item_tiles, rank, tile), BF16)], "q", *gram, old)
    kernel = functools.partial(y_kernel, 0)
    firsts = across(call(kernel, [y_bf16], "y_first", q, resid, flops=half_flops))
    kernel = functools.partial(y_kernel, half)
    seconds = across(call(kernel, [y_bf16], "y_second", q, resid, flops=half_flops))
    y_hat = user_step(firsts, seconds, True)
    left, user_dir = call(
        functools.partial(left_kernel, radius, math.sqrt(users)),
        [((users_dev, 3 * rank), BF16), ((rank, users_dev), F32)],
        "left",
        y_hat,
        a_t,
        flops=1 << 30,
    )
    z, z_share, (left, user_dir) = item_step(y_hat, BF16, (left, user_dir))

    grams = across(call(gram_kernel, [square], "gram", z))
    item_dir, losses = call(
        functools.partial(last_kernel, math.sqrt(items)),
        [((rank, share), F32), ((cap, tile), F32)],
        "loss",
        slots,
        *grams,
        z,
        z_share,
        ratings,
        left,
        bq,
        hbm=1,
        scratch_shapes=[
            pltpu.VMEM((item_tiles, 3 * rank, tile), BF16),
            pltpu.SMEM((3, cap), jnp.int32),
            pltpu.SemaphoreType.DMA,
        ],
    )
    return (user_dir, item_dir, losses[None, None])


def solution(mesh):
    return jax.shard_map(
        shards,
        mesh=mesh,
        in_specs=(
            P("user", "item", None, None, None),
            P("user", "item", None),
            P("user", "item", None),
            P("user", "item"),
            P(None, "user"),
            P(None, ("item", "user")),
            P(None, ("item", "user")),
        ),
        out_specs=(P(None, "user"), P(None, ("item", "user")), P("user", "item", None, None)),
        check_vma=False,
    )
```

```python
import functools
import math

import jax
import jax.numpy as jnp
from jax import lax
from jax.experimental import pallas as pl
from jax.experimental.pallas import tpu as pltpu
from jax.sharding import PartitionSpec as P

ITERS = 2
F32 = jnp.float32
BF16 = jnp.bfloat16
VMEM = pl.BlockSpec(memory_space=pltpu.VMEM)
SMEM = pl.BlockSpec(memory_space=pltpu.SMEM)
NT = (((1,), (1,)), ((), ()))
NN = (((1,), (0,)), ((), ()))


def xor_pairs(size, mask):
    return [(i, i ^ mask) for i in range(size)]


def bit_groups(size):
    bits = size.bit_length() - 1
    groups, at = [], 0
    while at < bits:
        width = 1 if at < 2 else min(2, bits - at)
        groups.append((at, width))
        at += width
    return groups


def position_of(index, size):
    place = index * 0
    for at, width in bit_groups(size):
        place = place * (1 << width) + ((index >> at) & ((1 << width) - 1))
    return place


def gather_blocks(held, axis, size, groups, before=None):
    for number, (at, width) in enumerate(reversed(groups)):
        if before is not None:
            held = before(number - len(groups), held)
        got = [held]
        for k in range(1, 1 << width):
            got.append(lax.ppermute(held, axis, xor_pairs(size, k << at)))
        held = jnp.concatenate(got, axis=0)
    return held


def reduce_blocks(near, far, axis, size, kind):
    groups = bit_groups(size)
    other = lax.ppermute(far.astype(kind), axis, xor_pairs(size, 1))
    parts = near.astype(F32) + other.astype(F32)
    for at, width in groups[1:-1]:
        ways = 1 << width
        pieces = parts.reshape((ways, parts.shape[0] // ways) + parts.shape[1:])
        total = pieces[0].astype(F32)
        got = [
            lax.ppermute(pieces[k].astype(kind), axis, xor_pairs(size, k << at))
            for k in range(1, ways)
        ]
        for piece in got:
            total = total + piece.astype(F32)
        parts = total
    at, width = groups[-1]
    mine = parts.astype(kind)
    total = mine.astype(F32)
    got = [lax.ppermute(mine, axis, xor_pairs(size, k << at)) for k in range(1, 1 << width)]
    for k, piece in enumerate(got, 1):
        total = total + jnp.stack([piece[j ^ k] for j in range(1 << width)]).astype(F32)
    return total


def y_of(q_cat, r_ref, at, users):
    return lax.dot_general(
        q_cat, r_ref[at : at + users, :], NT, preferred_element_type=F32
    )


def cat_tiles(ref, rows):
    return jnp.concatenate([ref[t, rows, :] for t in range(ref.shape[0])], axis=1)


def prepare_kernel(a_ref, at_ref, r_ref):
    tile = 128

    def clear(i, carry):
        r_ref[pl.ds(pl.multiple_of(i * tile, tile), tile), :] = jnp.zeros(
            (tile, r_ref.shape[1]), BF16
        )
        return carry

    lax.fori_loop(0, r_ref.shape[0] // tile, clear, 0)
    for t in range(at_ref.shape[0] // tile):
        cols = slice(t * tile, (t + 1) * tile)
        at_ref[cols, :] = a_ref[:, cols].astype(F32).T.astype(BF16)


def first_kernel(slot_ref, vals_ref, at_ref, bq_ref, _, r_ref, y_ref):
    tile = vals_ref.shape[1]
    rank = bq_ref.shape[1] // 2
    count = slot_ref[2, 0]
    group = math.gcd(vals_ref.shape[0], 64)

    def body(i, carry):
        for j in range(group):
            slot = i * group + j
            row = pl.multiple_of(slot_ref[0, slot] * tile, tile)
            pos = slot_ref[1, slot]
            pred = lax.dot_general(
                at_ref[pl.ds(row, tile), :],
                bq_ref[pos, :rank, :],
                NN,
                preferred_element_type=F32,
            )
            kept = jnp.where(slot < count, 1.0, 0.0)
            resid = (pred - vals_ref[slot].astype(F32)) * kept
            r_ref[pl.ds(row, tile), pl.ds(pl.multiple_of(pos * tile, tile), tile)] = resid.astype(
                BF16
            )
        return carry

    lax.fori_loop(0, (count + group - 1) // group, body, 0)
    y_ref[...] = y_of(cat_tiles(bq_ref, slice(rank, 2 * rank)), r_ref, 0, y_ref.shape[1])


def omega_kernel(at, bq_ref, r_ref, y_ref):
    rank = bq_ref.shape[1] // 2
    y_ref[...] = y_of(cat_tiles(bq_ref, slice(rank, 2 * rank)), r_ref, at, y_ref.shape[1])


def z_of(y, r_ref, at, z_ref, first, old_ref):
    tile = z_ref.shape[2]
    users = y.shape[1]
    wide = math.gcd(z_ref.shape[0], 8)
    for i in range(0, z_ref.shape[0], wide):
        z = lax.dot_general(
            y,
            r_ref[at : at + users, (first + i) * tile : (first + i + wide) * tile],
            NN,
            preferred_element_type=F32,
        )
        for j in range(wide):
            part = z[:, j * tile : (j + 1) * tile]
            if old_ref is not None:
                part = part + old_ref[first + i + j]
            z_ref[i + j] = part.astype(z_ref.dtype)


def exact_dot(left, right, dims):
    return lax.dot_general(
        left, right, dims, precision=lax.Precision.HIGHEST, preferred_element_type=F32
    )


def y_gram_kernel(ya_ref, yb_ref, y_ref, g_ref):
    y = ya_ref[...].astype(F32) + yb_ref[...].astype(F32)
    y_ref[...] = y
    g_ref[...] = exact_dot(y, y, NT)


def y_gram_more_kernel(ya_ref, yb_ref, old_ref, y_ref, g_ref):
    y = ya_ref[...].astype(F32) + yb_ref[...].astype(F32)
    y_ref[...] = y
    g_ref[...] = old_ref[...] + exact_dot(y, y, NT)


def y_hat_kernel(g_ref, y_0, y_1, out_ref):
    (inverse,) = chol_inverse([g_ref[...]])
    half = y_0.shape[1]
    out_ref[:, :half] = apply_wide(inverse, y_0[...])
    out_ref[:, half:] = apply_wide(inverse, y_1[...])


def y_near_hat_kernel(g_ref, y_0, ya_ref, yb_ref, out_ref):
    gram = g_ref[...]
    rows = lax.broadcasted_iota(jnp.int32, gram.shape, 0)
    diagonal = rows == lax.broadcasted_iota(jnp.int32, gram.shape, 1)
    (inverse,) = chol_inverse([gram + jnp.where(diagonal, gram * 1e-6 + 1e-30, 0.0)])
    half = y_0.shape[1]
    out_ref[:, :half] = apply_wide(inverse, y_0[...])
    out_ref[:, half:] = apply_wide(inverse, ya_ref[...] + yb_ref[...])


def z_kernel(first, y_ref, r_ref, z_ref):
    z_of(y_ref[...].astype(BF16), r_ref, 0, z_ref, first, None)


def gram_kernel(z_ref, g_ref):
    z = cat_tiles(z_ref, slice(None))
    if z.dtype == F32:
        g_ref[...] = exact_dot(z, z, NT)
    else:
        g_ref[...] = lax.dot_general(z, z, NT, preferred_element_type=F32)


def chol_inverse(grams):
    rank = grams[0].shape[0]
    wide = 8
    blocks = rank // wide
    rows = lax.broadcasted_iota(jnp.int32, (wide, 2 * rank), 0)
    lanes = lax.broadcasted_iota(jnp.int32, (wide, 2 * rank), 1)
    mats = []
    for g in grams:
        padded = jnp.concatenate([g, jnp.zeros_like(g)], axis=1)
        mats.append(
            [
                jnp.where(lanes == rows + (rank + i * wide), 1.0, padded[i * wide : (i + 1) * wide])
                for i in range(blocks)
            ]
        )
    for p in range(blocks):
        below = range(p, blocks)
        cols = [
            [
                {
                    i: jnp.broadcast_to(
                        mat[i][:, p * wide + k : p * wide + k + 1], (wide, 2 * rank)
                    )
                    for i in below
                }
                for k in range(wide)
            ]
            for mat in mats
        ]
        for k in range(0, wide, 2):
            for mat, col in zip(mats, cols):
                d = col[k][p][k : k + 1, :]
                e = col[k][p][k + 1 : k + 2, :]
                f = col[k + 1][p][k + 1 : k + 2, :]
                first = 1.0 / d
                second = d / (d * f - e * e)
                ratio = e * first
                row = mat[p][k : k + 1, :] * first
                next_row = mat[p][k + 1 : k + 2, :] - mat[p][k : k + 1, :] * ratio
                next_scaled = next_row * second
                one, two = {}, {}
                for i in below:
                    one[i] = col[k][i]
                    two[i] = col[k + 1][i] - col[k][i] * ratio
                    if i == p:
                        one[i] = jnp.where(rows > k, one[i], 0.0)
                        two[i] = jnp.where(rows > k + 1, two[i], 0.0)
                heads = {}
                for q in range(k + 2, wide):
                    top = col[q][p][k : k + 1, :]
                    heads[q] = (
                        top * first,
                        (col[q][p][k + 1 : k + 2, :] - top * ratio) * second,
                    )
                for i in below:
                    mat[i] = mat[i] - one[i] * row - two[i] * next_scaled
                    for q in range(k + 2, wide):
                        col[q][i] = col[q][i] - one[i] * heads[q][0] - two[i] * heads[q][1]
    result = []
    for mat in mats:
        out = []
        for i in range(blocks):
            diagonal = jnp.sum(
                jnp.where(lanes == rows + i * wide, mat[i], 0.0), axis=1, keepdims=True
            )
            out.append(mat[i][:, rank:] * lax.rsqrt(diagonal))
        result.append(jnp.concatenate(out, axis=0))
    return result


def two_parts(mat):
    high = mat.astype(BF16)
    return high, (mat - high.astype(F32)).astype(BF16)


def apply_inverse(inverse, mat):
    high, low = two_parts(inverse)
    return lax.dot_general(
        jnp.concatenate([high, low], axis=1),
        jnp.concatenate([mat, mat], axis=0),
        NN,
        preferred_element_type=F32,
    )


def apply_wide(inverse, mat):
    high, low = two_parts(inverse)
    part, rest = two_parts(mat)
    return lax.dot_general(
        jnp.concatenate([high, low, high], axis=1),
        jnp.concatenate([part, part, rest], axis=0),
        NN,
        preferred_element_type=F32,
    )


def q_kernel(ga_ref, gb_ref, z_ref, q_ref):
    (inverse,) = chol_inverse([ga_ref[...] + gb_ref[...]])
    for t in range(z_ref.shape[0]):
        q_ref[t] = apply_wide(inverse, z_ref[t]).astype(BF16)


def y_kernel(at, q_ref, r_ref, y_ref):
    y = y_of(cat_tiles(q_ref, slice(None)), r_ref, at, y_ref.shape[1])
    y_ref[...] = y.astype(y_ref.dtype)


def left_kernel(radius, user_scale, y_ref, at_ref, left_ref, user_ref):
    tile = 128
    user_ref[...] = y_ref[...] * user_scale
    for t in range(0, y_ref.shape[1], tile):
        rows = slice(t, t + tile)
        turned = (y_ref[:, rows].astype(BF16).astype(F32) * (-0.5 * radius)).T
        high, low = two_parts(turned)
        half = at_ref[rows, :].astype(F32) * 0.5
        left_ref[rows, :] = jnp.concatenate([half.astype(BF16), high, low], axis=1)


def last_kernel(
    item_scale,
    slot_any,
    ga_ref,
    gb_ref,
    z_ref,
    share_ref,
    vals_ref,
    left,
    bq_ref,
    item_ref,
    loss_ref,
    right,
    slot_ref,
    slot_sem,
):
    slot_copy = pltpu.make_async_copy(slot_any, slot_ref, slot_sem)
    slot_copy.start()
    tile = vals_ref.shape[1]
    rank = z_ref.shape[1]
    (z_inv,) = chol_inverse([ga_ref[...] + gb_ref[...]])
    for t in range(z_ref.shape[0]):
        q = apply_inverse(z_inv, z_ref[t]).astype(BF16)
        right[t, :rank] = bq_ref[t, :rank, :]
        right[t, rank : 2 * rank] = q
        right[t, 2 * rank : 3 * rank] = q
    item_ref[...] = apply_wide(z_inv, share_ref[...]) * item_scale
    loss_ref[...] = jnp.zeros_like(loss_ref)
    slot_copy.wait()
    count = slot_ref[2, 0]
    many = math.gcd(vals_ref.shape[0], 64)
    few = math.gcd(many, 8)
    place = lax.broadcasted_iota(jnp.int32, (few, tile), 0)

    def losses(start, slots):
        for g in range(0, slots, few):
            at = pl.multiple_of(start + g, few)
            sums = []
            for j in range(few):
                slot = at + j
                row = pl.multiple_of(slot_ref[0, slot] * tile, tile)
                fresh = lax.dot_general(
                    left[pl.ds(row, tile), :],
                    right[slot_ref[1, slot]],
                    NN,
                    preferred_element_type=F32,
                )
                fresh = fresh - vals_ref[slot].astype(F32)
                sums.append(jnp.sum(fresh * fresh, axis=-1))
            total = jnp.where(place + at < count, jnp.stack(sums, axis=0), 0.0)
            loss_ref[pl.ds(at, few), :] = total * (1.0 / tile)

    def loop(start, stop, slots):
        def body(i, carry):
            losses(start + i * slots, slots)
            return carry

        return lax.fori_loop(0, (stop - start) // slots, body, 0)

    whole = count // many * many
    some = math.gcd(many, 16)
    loop(0, whole, many)
    loop(whole, (count + some - 1) // some * some, some)


def shards(tile_vals, tile_row, tile_col, tile_count, fac_a, fac_b, omega):
    ratings = tile_vals[0, 0]
    cap, tile, _ = ratings.shape
    rank, users_dev = fac_a.shape
    share = fac_b.shape[1]
    n_user = lax.axis_size("user")
    n_item = lax.axis_size("item")
    items_dev = share * n_user
    item_tiles = items_dev // tile
    users, items = users_dev * n_user, items_dev * n_item
    radius = math.sqrt(users * items / rank)
    me = lax.axis_index("user").astype(jnp.int32)

    by_tile = share == tile
    if not by_tile:
        order = position_of(jnp.arange(n_user, dtype=jnp.int32) ^ me, n_user)

    def to_tiles(blocks):
        if by_tile:
            return blocks
        blocks = blocks[order]
        wide = blocks.transpose(1, 0, 2).reshape(blocks.shape[1], item_tiles, tile)
        return wide.transpose(1, 0, 2)

    def to_blocks(tiles):
        if by_tile:
            return tiles
        wide = tiles.transpose(1, 0, 2).reshape(tiles.shape[1], n_user, share)
        return jnp.zeros((n_user, tiles.shape[1], share), tiles.dtype).at[order].set(
            wide.transpose(1, 0, 2)
        )

    def across(mine):
        bit = 1
        while True:
            other = lax.ppermute(mine, "item", xor_pairs(n_item, bit))
            bit *= 2
            if bit >= n_item:
                return mine, other
            mine = (mine.astype(F32) + other.astype(F32)).astype(mine.dtype)

    def reduced(near, far, kind, work=()):
        if not by_tile:
            near, far = jnp.split(to_blocks(jnp.concatenate([near, far.astype(F32)])), 2)
        total = reduce_blocks(near, far, "user", n_user, kind)
        work = list(work)

        def before(number, held):
            if number == -1 and work:
                held, work[:] = lax.optimization_barrier((held, list(work)))
            return held

        groups = bit_groups(n_user)[:-1]
        z = gather_blocks(total.astype(kind), "user", n_user, groups, before)
        return to_tiles(z), total[0], work

    def call(kernel, outs, name, *args, smem=0, hbm=0, flops=0, vmem=16, **more):
        outs = [jax.ShapeDtypeStruct(shape, dtype) for shape, dtype in outs]
        got = pl.pallas_call(
            kernel,
            out_shape=outs,
            in_specs=[SMEM] * smem
            + [pl.BlockSpec(memory_space=pl.ANY)] * hbm
            + [VMEM] * (len(args) - smem - hbm),
            out_specs=[VMEM] * len(outs),
            compiler_params=pltpu.CompilerParams(vmem_limit_bytes=vmem << 20),
            cost_estimate=pl.CostEstimate(flops=flops, bytes_accessed=1 << 16, transcendentals=0),
            name=name,
            **more,
        )(*args)
        return got[0] if len(outs) == 1 else got

    half = users_dev // 2
    r_shape = ((users_dev, items_dev), BF16)
    y_f32, y_bf16 = ((rank, half), F32), ((rank, half), BF16)
    some = users_dev // 4
    y_some, y_rest = ((rank, some), F32), ((rank, users_dev - some), F32)
    half_flops = 2 * rank * half * items_dev

    work = [fac_a, tile_row, tile_col, tile_count]

    def before(number, held):
        if number == 1 - len(bit_groups(n_user)):
            held, work[:] = lax.optimization_barrier((held, list(work)))
            user_factor, rows, cols, count = work
            cols = cols[0, 0]
            if by_tile:
                cols = position_of(cols ^ me, n_user)
            slots = jnp.stack([rows[0, 0], cols, jnp.broadcast_to(count[0, 0], (cap,))])
            a_t, cleared = call(
                prepare_kernel,
                [((users_dev, rank), BF16), r_shape],
                "prepare",
                user_factor,
                flops=1 << 31,
            )
            work[:] = [a_t, slots, cleared]
        elif number == -1:
            held, work[:2] = lax.optimization_barrier((held, list(work[:2])))
        return held

    both = lax.optimization_barrier(jnp.concatenate([fac_b, omega], axis=0))
    bq = to_tiles(gather_blocks(both[None], "user", n_user, bit_groups(n_user), before))
    a_t, slots, cleared = work

    def over_users(part):
        for at, width in bit_groups(n_user):
            terms = [part]
            for k in range(1, 1 << width):
                terms.append(lax.ppermute(part, "user", xor_pairs(n_user, k << at)))
            while len(terms) > 1:
                terms = [a + b for a, b in zip(terms[::2], terms[1::2])]
            part = terms[0]
        return part

    square = ((rank, rank), F32)

    def user_step(firsts, seconds, exact):
        summed = [(firsts[0].shape, F32), square]
        y_0, gram = call(y_gram_kernel, summed, "y_gram", *firsts, flops=half_flops)
        whole = [((rank, users_dev), F32)]
        if not exact:
            return call(y_near_hat_kernel, whole, "y_hat", over_users(gram), y_0, *seconds)
        y_1, gram = call(y_gram_more_kernel, [y_f32, square], "y_gram_more", *seconds, gram)
        return call(y_hat_kernel, whole, "y_hat", over_users(gram), y_0, y_1)

    def item_step(y_hat, kind, work=()):
        near, far = item_tiles // 2, item_tiles - item_tiles // 2
        kernel = functools.partial(z_kernel, near)
        later = call(
            kernel, [((far, rank, tile), kind)], "z_far", y_hat, resid, flops=half_flops
        )
        kernel = functools.partial(z_kernel, 0)
        sooner = call(
            kernel, [((near, rank, tile), F32)], "z_near", y_hat, resid, flops=half_flops
        )
        return reduced(sooner, later, kind, work)

    resid, y_0 = call(
        first_kernel,
        [r_shape, y_some],
        "resid_y",
        slots,
        ratings,
        a_t,
        bq,
        cleared,
        smem=1,
        input_output_aliases={4: 0},
    )
    firsts = across(y_0)
    kernel = functools.partial(omega_kernel, some)
    y_1 = call(kernel, [y_rest], "y_omega", bq, resid, flops=half_flops)
    firsts, y_1 = lax.optimization_barrier((firsts, y_1))
    seconds = across(y_1)
    old, _, _ = item_step(user_step(firsts, seconds, False), F32)

    gram = across(call(gram_kernel, [square], "gram", old))
    q = call(q_kernel, [((item_tiles, rank, tile), BF16)], "q", *gram, old)
    kernel = functools.partial(y_kernel, 0)
    firsts = across(call(kernel, [y_bf16], "y_first", q, resid, flops=half_flops))
    kernel = functools.partial(y_kernel, half)
    seconds = across(call(kernel, [y_bf16], "y_second", q, resid, flops=half_flops))
    y_hat = user_step(firsts, seconds, True)
    left, user_dir = call(
        functools.partial(left_kernel, radius, math.sqrt(users)),
        [((users_dev, 3 * rank), BF16), ((rank, users_dev), F32)],
        "left",
        y_hat,
        a_t,
        flops=1 << 30,
    )
    z, z_share, (left, user_dir) = item_step(y_hat, BF16, (left, user_dir))

    grams = across(call(gram_kernel, [square], "gram", z))
    item_dir, losses = call(
        functools.partial(last_kernel, math.sqrt(items)),
        [((rank, share), F32), ((cap, tile), F32)],
        "loss",
        slots,
        *grams,
        z,
        z_share,
        ratings,
        left,
        bq,
        hbm=1,
        scratch_shapes=[
            pltpu.VMEM((item_tiles, 3 * rank, tile), BF16),
            pltpu.SMEM((3, cap), jnp.int32),
            pltpu.SemaphoreType.DMA,
        ],
    )
    return (user_dir, item_dir, losses[None, None])


def solution(mesh):
    return jax.shard_map(
        shards,
        mesh=mesh,
        in_specs=(
            P("user", "item", None, None, None),
            P("user", "item", None),
            P("user", "item", None),
            P("user", "item"),
            P(None, "user"),
            P(None, ("item", "user")),
            P(None, ("item", "user")),
        ),
        out_specs=(P(None, "user"), P(None, ("item", "user")), P("user", "item", None, None)),
        check_vma=False,
    )
```
